32 devices in a mesh: wide: 8 (over z, x), narrow: 4 (over y, core).
Axes of the slice: x: 2, y: 2, z: 4, core: 2. Of those that a mesh axis runs over, the one named last changes fastest.
Arguments:
- tokens: bfloat16 [64, 1024, 768], P(('wide', 'narrow')), may hold values from -6 to 6
- cotangent: bfloat16 [64, 1024, 768], P(('wide', 'narrow')), may hold values from -6 to 6
- row_kind: int32 [64], P(('wide', 'narrow')), may hold values from 0 to 1
- grad_mask: int32 [64, 1024], P(('wide', 'narrow')), may hold values 0 or 1
- w_qkv: bfloat16 [768, 2304], P('wide'), may hold values from -0.3125 to 0.3125
- w_out: bfloat16 [768, 768], P('wide'), may hold values from -0.625 to 0.625
- w_in: bfloat16 [768, 3072], P('wide'), may hold values from -0.21875 to 0.21875
- w_back: bfloat16 [3072, 768], P('wide'), may hold values from -0.109375 to 0.109375
- norm_gain: bfloat16 [2, 768], P(None, 'wide'), may hold values from 0.5 to 1.5
- norm_shift: bfloat16 [2, 768], P(None, 'wide'), may hold values from -1 to 1
- proj_bias: bfloat16 [4, 768], P(None, 'wide'), may hold values from -1 to 1
- ffn_bias: bfloat16 [3072], P('wide'), may hold values from -1 to 1
Outputs:
- layer_out: bfloat16 [64, 1024, 768], P(('wide', 'narrow'))
- input_grad: float32 [64, 1024, 768], P(('wide', 'narrow'))
- grad_qkv: float32 [768, 2304], P('wide')
- grad_out: float32 [768, 768], P('wide')
- grad_in: float32 [768, 3072], P('wide')
- grad_back: float32 [3072, 768], P('wide')
- grad_gain: float32 [2, 768], P(None, 'wide')
- grad_shift: float32 [2, 768], P(None, 'wide')
- grad_proj_bias: float32 [4, 768], P(None, 'wide')
- grad_ffn_bias: float32 [3072], P('wide')
The draws below stay inside these ranges and needn't reach their ends.
All inputs are finite; a program needn't handle non-finite values. No bound on the sum of `grad_mask` on one device may be relied on, other than what follows from the above.
Results may differ from the reference program's by a relative error of at most 0.02.
Values may be sent and summed in bfloat16 or wider, within the bound.
No kernel may reach another device: no remote copies, remote signals or barrier semaphores. Data moves between devices by JAX's collectives and lax.ppermute only.
A program may use at most 384 MiB of HBM per device.

```python
import jax
import jax.numpy as jnp
from jax import lax

D = 768
HEADS = 12
HEAD_DIM = 64
FF = 3072
SEQ = 1024
BATCH = 64


def plant(drawn, key, low, largest):
    dims = drawn.shape
    index_at = [jax.random.randint(jax.random.fold_in(key, axis), (), 0, dims[axis]) for axis in range(len(dims))]
    drawn = drawn.at[tuple(index_at)].set(low)
    longest = dims.index(max(dims))
    index_at[longest] = (index_at[longest] + 1) % dims[longest]
    return drawn.at[tuple(index_at)].set(largest)


def levels(rng, shape, pieces, low, top_value):
    def one(position, parts):
        heights = jax.random.uniform(jax.random.fold_in(jax.random.fold_in(rng, 6), position), (parts,), jnp.float32, low / len(pieces), top_value / len(pieces))
        return jnp.repeat(jnp.exp(heights), shape[position] // parts).reshape((-1,) + (1,) * (len(shape) - position - 1))

    level = one(*pieces[0])
    for cut in pieces[1:]:
        level = level * one(*cut)
    return level


def noise(key, extent, deviation, reach, split=(), held_as=jnp.bfloat16):
    entries = deviation * jax.random.normal(key, extent, jnp.float32)
    if split:
        entries = entries * levels(key, extent, split, -0.22, 0.18)
    return jnp.clip(entries, -reach, reach).astype(held_as)


def setup_inputs(seed: int = 0) -> dict:
    key_list = jax.random.split(jax.random.key(seed), 13)
    tokens = noise(key_list[0], (BATCH, SEQ, D), 1.0, 6.0, ((0, 32),))
    cotangent = noise(key_list[1], (BATCH, SEQ, D), 1.0, 6.0, ((0, 32),))
    row_kind = plant(jax.random.randint(key_list[2], (BATCH,), 0, 2), jax.random.fold_in(key_list[2], 1), 0, 1).astype(jnp.int32)
    grad_mask = plant((jax.random.randint(key_list[3], (BATCH, SEQ), 0, 100) < 15).astype(jnp.int32), jax.random.fold_in(key_list[3], 1), 0, 1)
    w_qkv = noise(key_list[4], (D, 3 * D), (D // 2) ** -0.5, 0.3125, ((0, 8),))
    w_out = noise(key_list[5], (D, D), (D // 8) ** -0.5, 0.625, ((0, 8),))
    w_in = noise(key_list[6], (D, FF), D ** -0.5, 0.21875, ((0, 8),))
    w_back = noise(key_list[7], (FF, D), FF ** -0.5, 0.109375, ((0, 8),))
    norm_gain = jnp.clip(1.0 + 0.1 * jax.random.normal(key_list[8], (2, D), jnp.float32), 0.5, 1.5).astype(jnp.bfloat16)
    norm_shift = noise(key_list[9], (2, D), 0.2, 1.0, ((1, 8),))
    proj_bias = noise(key_list[10], (4, D), 0.2, 1.0, ((1, 8),))
    ffn_bias = noise(key_list[11], (FF,), 0.2, 1.0, ((0, 8),))
    return dict(tokens=tokens, cotangent=cotangent, row_kind=row_kind, grad_mask=grad_mask, w_qkv=w_qkv, w_out=w_out, w_in=w_in, w_back=w_back, norm_gain=norm_gain, norm_shift=norm_shift, proj_bias=proj_bias, ffn_bias=ffn_bias)


@jax.custom_vjp
def low(v):
    return lax.optimization_barrier(v.astype(jnp.bfloat16)).astype(jnp.float32)

@jax.custom_vjp
def low_back(v):
    return v

def low_keep(v):
    return (low(v), None)

def low_pass(kept, grad):
    return (grad,)

def back_keep(v):
    return (v, None)

def back_low(kept, grad):
    return (low(grad),)
low.defvjp(low_keep, low_pass)
low_back.defvjp(back_keep, back_low)
EPSILON = 1e-05
HIGHEST = lax.Precision.HIGHEST

def normalize(values, gain, shift):
    centre = lax.optimization_barrier(jnp.mean(values, axis=-1, keepdims=True))
    centred = values - centre
    variance = lax.optimization_barrier(jnp.mean(centred * centred, axis=-1, keepdims=True))
    return centred * lax.rsqrt(variance + EPSILON) * gain + shift

def smooth_gate(values):
    return 0.5 * values * (1.0 + jnp.tanh(0.7978845608028654 * (values + 0.044715 * values * values * values)))

def layer(inputs, w_qkv, w_out, w_in, w_back, norm_gain, norm_shift, proj_bias, ffn_bias):
    length = inputs.shape[0]
    width = inputs.shape[1]
    normed_one = low(normalize(inputs, norm_gain[0], norm_shift[0]))
    zero_bias = jnp.zeros_like(proj_bias[0])
    qkv_bias = jnp.concatenate([proj_bias[0], zero_bias, proj_bias[1]])
    projected = low(low_back(jnp.dot(normed_one, w_qkv, precision=HIGHEST) + qkv_bias))
    split_heads = projected.reshape(length, 3, HEADS, HEAD_DIM)
    query = split_heads[:, 0]
    keys = split_heads[:, 1]
    value = split_heads[:, 2]
    scores = low_back(jnp.einsum('qhd,khd->hqk', query, keys, precision=HIGHEST) * HEAD_DIM ** (-0.5))
    peak = lax.optimization_barrier(jnp.max(scores, axis=-1, keepdims=True))
    expo = jnp.exp(scores - peak)
    probs = low(expo / lax.optimization_barrier(jnp.sum(expo, axis=-1, keepdims=True)))
    mixed = jnp.einsum('hqk,khd->qhd', probs, value, precision=HIGHEST).reshape(length, width)
    mixed = low(low_back(mixed))
    branch_attn = low_back(jnp.dot(mixed, w_out, precision=HIGHEST) + proj_bias[2])
    hidden = inputs + branch_attn
    normed_two = low(normalize(hidden, norm_gain[1], norm_shift[1]))
    pre_act = low_back(jnp.dot(normed_two, w_in, precision=HIGHEST) + ffn_bias)
    active = low(smooth_gate(pre_act))
    branch_ffn = low_back(jnp.dot(active, w_back, precision=HIGHEST) + proj_bias[3])
    return hidden + branch_ffn

def reference(tokens, cotangent, row_kind, grad_mask, w_qkv, w_out, w_in, w_back, norm_gain, norm_shift, proj_bias, ffn_bias):
    params = tuple((p.astype(jnp.float32) for p in (w_qkv, w_out, w_in, w_back, norm_gain, norm_shift, proj_bias, ffn_bias)))
    keep = jnp.where(row_kind[:, None] == 1, jnp.ones(grad_mask.shape, jnp.float32), grad_mask.astype(jnp.float32))

    def per_sequence(totals, members):
        sequence, grad_seq, kept = members
        result, pull = jax.vjp(layer, sequence.astype(jnp.float32), *params)
        grads = pull(grad_seq.astype(jnp.float32) * kept[:, None])
        totals = tuple((t + g for t, g in zip(totals, grads[1:])))
        return (totals, (result.astype(jnp.bfloat16), grads[0]))
    initial = tuple((jnp.zeros(p.shape, jnp.float32) for p in params))
    totals, (outputs, input_grad) = lax.scan(per_sequence, initial, (tokens, cotangent, keep))
    return (outputs, input_grad, totals[0], totals[1], totals[2], totals[3], totals[4], totals[5], totals[6], totals[7])
```

```python
import jax, jax.numpy as jnp, functools
from jax import lax
from jax.experimental import pallas as pl
from jax.experimental.pallas import tpu as pltpu
F32=jnp.float32; BF=jnp.bfloat16
NT=(((1,),(1,)),((),())); NN=(((1,),(0,)),((),())); TN=(((0,),(0,)),((),()))
def dot(a,b,d): return lax.dot_general(a,b,d,preferred_element_type=F32)

def pieces(x):
    hi=x.astype(BF); r=x-hi.astype(F32); mid=r.astype(BF); lo=(r-mid.astype(F32)).astype(BF)
    return hi,mid,lo

def spread(x, lane):
    hi,mid,lo=pieces(x)
    at=lane & 63
    z=jnp.zeros_like(x)
    return jnp.where(at==0,hi.astype(F32),jnp.where(at==1,mid.astype(F32),jnp.where(at==2,lo.astype(F32),z))).astype(BF)

def fwd_kernel(bq, q_ref, k_ref, v_ref, o_ref, l_ref):
    length=q_ref.shape[0]
    lane=lax.broadcasted_iota(jnp.int32,(length,128),1)
    left=lane<64
    lq=lax.broadcasted_iota(jnp.int32,(bq,128),1); leftq=lq<64
    v=v_ref[...].astype(F32)
    ones=jnp.ones_like(v)
    va=jnp.where(left,v,ones).astype(BF); vb=jnp.where(left,ones,v).astype(BF)
    k=k_ref[...]
    for i in range(length//bq):
        q=q_ref[pl.ds(i*bq,bq),:].astype(F32)*0.125
        zero=jnp.zeros_like(q)
        qa=jnp.where(leftq,q,zero).astype(BF); qb=jnp.where(leftq,zero,q).astype(BF)
        outs=[]; peaks=[]
        for qq,vv in ((qa,va),(qb,vb)):
            s=dot(qq,k,NT)
            m=jnp.max(s,axis=1,keepdims=True)
            p=jnp.exp(s-m).astype(BF)
            outs.append(dot(p,vv,NN)); peaks.append(m)
        oa,ob=outs
        num=jnp.where(leftq,oa,ob); den=jnp.where(leftq,ob,oa)
        o_ref[pl.ds(i*bq,bq),:]=(num/pltpu.roll(den,64,1)).astype(BF)
        lse=jnp.where(leftq,peaks[1],peaks[0])+jnp.log(den)
        l_ref[pl.ds(i*bq,bq),:]=spread(lse,lq)

def attn_fwd(qkv, rows, bq=256):
    n=qkv.shape[0]; length=n//rows; width=qkv.shape[1]//3; pairs=width//128
    spec=lambda off: pl.BlockSpec((length,128),lambda s,p,off=off:(s,off+p))
    return pl.pallas_call(functools.partial(fwd_kernel,bq),grid=(rows,pairs),
        in_specs=[spec(0),spec(pairs),spec(2*pairs)],out_specs=[spec(0),spec(0)],
        out_shape=[jax.ShapeDtypeStruct((n,width),BF)]*2,
        compiler_params=pltpu.CompilerParams(vmem_limit_bytes=56<<20),
        cost_estimate=pl.CostEstimate(flops=4*n*length*width,bytes_accessed=n*width*10,transcendentals=n*length*width//64),
        name="attention_forward")(qkv,qkv,qkv)

def bwd_kernel(bq, q_ref,k_ref,v_ref,o_ref,l_ref,g_ref, gq_ref,gk_ref,gv_ref, ak,av):
    length=q_ref.shape[0]
    lane=lax.broadcasted_iota(jnp.int32,(length,128),1)
    left=lane<64; at=lane&63
    lq=lax.broadcasted_iota(jnp.int32,(bq,128),1); leftq=lq<64
    k=k_ref[...].astype(F32); v=v_ref[...].astype(F32)
    tail=jnp.where(at<3,-1.0,0.0).astype(F32)
    zero=jnp.zeros_like(k)
    kx=(jnp.where(left,k,tail).astype(BF),jnp.where(left,tail,k).astype(BF))
    km=(jnp.where(left,k,zero).astype(BF),jnp.where(left,zero,k).astype(BF))
    vx=(jnp.where(left,v,tail).astype(BF),jnp.where(left,tail,v).astype(BF))
    for i in range(length//bq):
        at_q=pl.ds(i*bq,bq)
        q=q_ref[at_q,:].astype(F32)*0.125
        l=l_ref[at_q,:].astype(F32)
        g=g_ref[at_q,:].astype(F32)
        zq=jnp.zeros_like(q)
        prod=g*o_ref[at_q,:].astype(F32)
        da=jnp.sum(jnp.where(leftq,prod,zq),axis=1,keepdims=True)
        db=jnp.sum(jnp.where(leftq,zq,prod),axis=1,keepdims=True)
        d=spread(jnp.where(leftq,db,da),lq).astype(F32)
        qx=(jnp.where(leftq,q,l).astype(BF),jnp.where(leftq,l,q).astype(BF))
        qm=(jnp.where(leftq,q,zq).astype(BF),jnp.where(leftq,zq,q).astype(BF))
        gx=(jnp.where(leftq,g,d).astype(BF),jnp.where(leftq,d,g).astype(BF))
        gm=(jnp.where(leftq,g,zq).astype(BF),jnp.where(leftq,zq,g).astype(BF))
        gq=None; gk=None; gv=None
        for h in range(2):
            p=jnp.exp(dot(kx[h],qx[h],NT))
            ds=(p*dot(vx[h],gx[h],NT)).astype(BF)
            tv=dot(p.astype(BF),gm[h],NN); tk=dot(ds,qm[h],NN); tq=dot(ds,km[h],TN)
            gq=tq if gq is None else gq+tq
            gk=tk if gk is None else gk+tk
            gv=tv if gv is None else gv+tv
        gq_ref[at_q,:]=(gq*0.125).astype(BF)
        if i==0: ak[...]=gk; av[...]=gv
        else: ak[...]+=gk; av[...]+=gv
    gk_ref[...]=ak[...].astype(BF); gv_ref[...]=av[...].astype(BF)

def attn_bwd(qkv,mixed,lse,gmixed,rows,bq=256):
    n=qkv.shape[0]; length=n//rows; width=qkv.shape[1]//3; pairs=width//128
    spec=lambda off: pl.BlockSpec((length,128),lambda s,p,off=off:(s,off+p))
    return pl.pallas_call(functools.partial(bwd_kernel,bq),grid=(rows,pairs),
        in_specs=[spec(0),spec(pairs),spec(2*pairs),spec(0),spec(0),spec(0)],out_specs=[spec(0)]*3,
        out_shape=[jax.ShapeDtypeStruct((n,width),BF)]*3,
        scratch_shapes=[pltpu.VMEM((length,128),F32)]*2,
        compiler_params=pltpu.CompilerParams(vmem_limit_bytes=56<<20),
        cost_estimate=pl.CostEstimate(flops=10*n*length*width,bytes_accessed=n*width*18,transcendentals=n*length*width//64),
        name="attention_backward")(qkv,qkv,qkv,mixed,lse,gmixed)

from jax.sharding import PartitionSpec as P

HEADS = 12


EPSILON = 1e-05
ROOT_TWO_PI = 0.7978845608028654
CUBIC = 0.044715


def normalize(values, gain, shift):
    centre = jnp.mean(values, axis=-1, keepdims=True)
    centred = values - centre
    variance = jnp.mean(centred * centred, axis=-1, keepdims=True)
    inv_std = lax.rsqrt(variance + EPSILON)
    scaled = centred * inv_std
    return (scaled, inv_std, scaled * gain + shift)


def smooth_gate(values):
    return (
        0.5 * values * (1.0 + jnp.tanh(ROOT_TWO_PI * (values + CUBIC * values * values * values)))
    )


def gate_slope(values):
    bent = jnp.tanh(ROOT_TWO_PI * (values + CUBIC * values * values * values))
    return 0.5 * (1.0 + bent) + 0.5 * values * (1.0 - bent * bent) * ROOT_TWO_PI * (
        1.0 + 3.0 * CUBIC * values * values
    )


def norm_back(grad_norm, scaled, inv_std, gain):
    grad_scaled = grad_norm * gain
    first_mean = jnp.mean(grad_scaled, axis=-1, keepdims=True)
    second_mean = jnp.mean(grad_scaled * scaled, axis=-1, keepdims=True)
    return inv_std * (grad_scaled - first_mean - scaled * second_mean)


def body(
    tokens,
    cotangent,
    row_kind,
    grad_mask,
    w_qkv,
    w_out,
    w_in,
    w_back,
    norm_gain,
    norm_shift,
    proj_bias,
    ffn_bias,
):
    rows, length, width = tokens.shape
    count = rows * length
    head_size = width // HEADS
    share = width // lax.axis_size("wide")
    packed = jnp.concatenate([norm_gain, norm_shift, proj_bias, ffn_bias.reshape(-1, share)])
    qkv_full = lax.all_gather(w_qkv, "wide", axis=0, tiled=True)
    small = lax.all_gather(packed, "wide", axis=0)
    out_full = lax.all_gather(w_out, "wide", axis=0, tiled=True)
    in_full = lax.all_gather(w_in, "wide", axis=0, tiled=True)
    back_full = lax.all_gather(w_back, "wide", axis=0, tiled=True)
    by_column = small[:, :8].transpose(1, 0, 2).reshape(8, width)
    gain_full, shift_full, bias_full = by_column[:2], by_column[2:4], by_column[4:8]
    ffn_bias_full = small[:, 8:].reshape(-1)
    gains = gain_full.astype(jnp.float32)
    shifts = shift_full.astype(jnp.float32)
    biases = bias_full.astype(jnp.float32)
    inputs = tokens.reshape(count, width).astype(jnp.float32)
    scaled_one, inv_one, normed = normalize(inputs, gains[0], shifts[0])
    normed_one = normed.astype(jnp.bfloat16)
    zero_bias = jnp.zeros((width,), jnp.float32)
    qkv_bias = jnp.concatenate([biases[0], zero_bias, biases[1]])
    projected = jnp.dot(normed_one, qkv_full, preferred_element_type=jnp.float32) + qkv_bias
    qkv = projected.astype(jnp.bfloat16)
    mixed_low, logsum = attn_fwd(qkv, rows, 512)
    hidden = inputs + jnp.dot(mixed_low, out_full, preferred_element_type=jnp.float32) + biases[2]
    scaled_two, inv_two, normed = normalize(hidden, gains[1], shifts[1])
    normed_two = normed.astype(jnp.bfloat16)
    pre_act = jnp.dot(
        normed_two, in_full, preferred_element_type=jnp.float32
    ) + ffn_bias_full.astype(jnp.float32)
    active = smooth_gate(pre_act).astype(jnp.bfloat16)
    result = hidden + jnp.dot(active, back_full, preferred_element_type=jnp.float32) + biases[3]
    layer_out = result.astype(jnp.bfloat16).reshape(rows, length, width)
    keep = jnp.where(
        row_kind[:, None] == 1,
        jnp.ones(grad_mask.shape, jnp.float32),
        grad_mask.astype(jnp.float32),
    )
    grad_result = (cotangent.astype(jnp.float32) * keep[:, :, None]).reshape(count, width)
    grad_ffn = grad_result.astype(jnp.bfloat16)
    grad_back = jnp.einsum("nf,nd->fd", active, grad_ffn, preferred_element_type=jnp.float32)
    bias_four = jnp.sum(grad_ffn.astype(jnp.float32), axis=0)
    grad_active = jnp.einsum("nd,fd->nf", grad_ffn, back_full, preferred_element_type=jnp.float32)
    grad_pre = (grad_active * gate_slope(pre_act)).astype(jnp.bfloat16)
    grad_in = jnp.einsum("nd,nf->df", normed_two, grad_pre, preferred_element_type=jnp.float32)
    grad_ffn_bias = jnp.sum(grad_pre.astype(jnp.float32), axis=0)
    grad_two = jnp.einsum("nf,df->nd", grad_pre, in_full, preferred_element_type=jnp.float32)
    gain_two = jnp.sum(grad_two * scaled_two, axis=0)
    shift_two = jnp.sum(grad_two, axis=0)
    grad_hidden = grad_result + norm_back(grad_two, scaled_two, inv_two, gains[1])
    in_share = lax.psum_scatter(
        grad_in.astype(jnp.bfloat16), "wide", scatter_dimension=0, tiled=True
    )
    back_share = lax.psum_scatter(
        grad_back.astype(jnp.bfloat16), "wide", scatter_dimension=0, tiled=True
    )
    grad_attn = grad_hidden.astype(jnp.bfloat16)
    grad_out = jnp.einsum("nc,nd->cd", mixed_low, grad_attn, preferred_element_type=jnp.float32)
    bias_three = jnp.sum(grad_attn.astype(jnp.float32), axis=0)
    grad_mixed = jnp.einsum("nd,cd->nc", grad_attn, out_full, preferred_element_type=jnp.float32)
    grad_proj = jnp.concatenate(
        attn_bwd(qkv, mixed_low, logsum, grad_mixed.astype(jnp.bfloat16), rows), axis=1
    )
    grad_qkv = jnp.einsum("nd,ne->de", normed_one, grad_proj, preferred_element_type=jnp.float32)
    column_sums = jnp.sum(grad_proj.astype(jnp.float32), axis=0)
    grad_one = jnp.einsum("ne,de->nd", grad_proj, qkv_full, preferred_element_type=jnp.float32)
    gain_one = jnp.sum(grad_one * scaled_one, axis=0)
    shift_one = jnp.sum(grad_one, axis=0)
    input_grad = grad_hidden + norm_back(grad_one, scaled_one, inv_one, gains[0])
    qkv_share = lax.psum_scatter(
        grad_qkv.astype(jnp.bfloat16), "wide", scatter_dimension=0, tiled=True
    )
    out_share = lax.psum_scatter(
        grad_out.astype(jnp.bfloat16), "wide", scatter_dimension=0, tiled=True
    )
    by_column = jnp.stack(
        [
            gain_one,
            gain_two,
            shift_one,
            shift_two,
            column_sums[:width],
            column_sums[2 * width :],
            bias_three,
            bias_four,
        ]
    )
    by_column = by_column.reshape(8, -1, share).transpose(1, 0, 2)
    small = jnp.concatenate([by_column, grad_ffn_bias.reshape(by_column.shape[0], -1, share)], axis=1)
    small = lax.psum(small.astype(jnp.bfloat16), ("wide", "narrow"))
    small = lax.dynamic_index_in_dim(small, lax.axis_index("wide"), 0, keepdims=False)
    small = small.astype(jnp.float32)
    summed = lax.psum((qkv_share, out_share, in_share, back_share), "narrow")
    summed = [part.astype(jnp.float32) for part in summed]
    return (
        layer_out,
        input_grad.reshape(rows, length, width),
        summed[0],
        summed[1],
        summed[2],
        summed[3],
        small[:2],
        small[2:4],
        small[4:8],
        small[8:].reshape(-1),
    )


def solution(mesh):
    in_specs = (
        P(("wide", "narrow"), None, None),
        P(("wide", "narrow"), None, None),
        P(("wide", "narrow")),
        P(("wide", "narrow"), None),
        P("wide", None),
        P("wide", None),
        P("wide", None),
        P("wide", None),
        P(None, "wide"),
        P(None, "wide"),
        P(None, "wide"),
        P("wide"),
    )
    out_specs = (
        P(("wide", "narrow"), None, None),
        P(("wide", "narrow"), None, None),
        P("wide", None),
        P("wide", None),
        P("wide", None),
        P("wide", None),
        P(None, "wide"),
        P(None, "wide"),
        P(None, "wide"),
        P("wide"),
    )
    return jax.shard_map(body, mesh=mesh, in_specs=in_specs, out_specs=out_specs, check_vma=False)
```

```python
import functools

import jax
import jax.numpy as jnp
from jax import lax
from jax.experimental import pallas as pl
from jax.experimental.pallas import tpu as pltpu
from jax.sharding import PartitionSpec as P

HEADS = 12
F32 = jnp.float32
BF = jnp.bfloat16
EPS = 1e-05
ROOT = 0.7978845608028654
CUBIC = 0.044715
NN = (((1,), (0,)), ((), ()))
NT = (((1,), (1,)), ((), ()))
TN = (((0,), (0,)), ((), ()))


def dot(a, b, dims):
    return lax.dot_general(a, b, dims, preferred_element_type=F32)


def spread(x, lane):
    hi = x.astype(BF).astype(F32)
    rest = x - hi
    mid = rest.astype(BF).astype(F32)
    at = lane & 63
    zero = jnp.zeros_like(x)
    picked = jnp.where(at == 0, hi, jnp.where(at == 1, mid, jnp.where(at == 2, rest - mid, zero)))
    return picked.astype(BF)

def fwd_kernel(bq, q_ref, k_ref, v_ref, o_ref, l_ref):
    length=q_ref.shape[0]
    lane=lax.broadcasted_iota(jnp.int32,(length,128),1)
    left=lane<64
    lq=lax.broadcasted_iota(jnp.int32,(bq,128),1); leftq=lq<64
    v=v_ref[...].astype(F32)
    ones=jnp.ones_like(v)
    va=jnp.where(left,v,ones).astype(BF); vb=jnp.where(left,ones,v).astype(BF)
    k=k_ref[...]
    for i in range(length//bq):
        q=q_ref[pl.ds(i*bq,bq),:].astype(F32)*0.125
        zero=jnp.zeros_like(q)
        qa=jnp.where(leftq,q,zero).astype(BF); qb=jnp.where(leftq,zero,q).astype(BF)
        outs=[]; peaks=[]
        for qq,vv in ((qa,va),(qb,vb)):
            s=dot(qq,k,NT)
            m=jnp.max(s,axis=1,keepdims=True)
            p=jnp.exp(s-m).astype(BF)
            outs.append(dot(p,vv,NN)); peaks.append(m)
        oa,ob=outs
        num=jnp.where(leftq,oa,ob); den=jnp.where(leftq,ob,oa)
        o_ref[pl.ds(i*bq,bq),:]=(num/pltpu.roll(den,64,1)).astype(BF)
        lse=jnp.where(leftq,peaks[1],peaks[0])+jnp.log(den)
        l_ref[pl.ds(i*bq,bq),:]=spread(lse,lq)


def attn_fwd(qkv, rows, bq=512):
    n = qkv.shape[0]
    length = n // rows
    width = qkv.shape[1] // 3
    pairs = width // 128

    def spec(off):
        return pl.BlockSpec((length, 128), lambda s, p: (s, off + p))

    return pl.pallas_call(
        functools.partial(fwd_kernel, bq),
        grid=(rows, pairs),
        in_specs=[spec(0), spec(pairs), spec(2 * pairs)],
        out_specs=[spec(0), spec(0)],
        out_shape=[jax.ShapeDtypeStruct((n, width), BF)] * 2,
        compiler_params=pltpu.CompilerParams(vmem_limit_bytes=56 << 20),
        cost_estimate=pl.CostEstimate(
            flops=30 * n * length * width,
            bytes_accessed=n * width * 10,
            transcendentals=n * length * width // 64,
        ),
        name="attention_forward",
    )(qkv, qkv, qkv)


def bwd_kernel(bq, q_ref,k_ref,v_ref,o_ref,l_ref,g_ref,out_ref,ak,av):
    length=q_ref.shape[0]
    part=out_ref.shape[1]//3
    start=pl.program_id(1)*128
    cols=[pl.ds(pl.multiple_of(start+j*part,128),128) for j in range(3)]
    lane=lax.broadcasted_iota(jnp.int32,(length,128),1)
    left=lane<64; at=lane&63
    lq=lax.broadcasted_iota(jnp.int32,(bq,128),1); leftq=lq<64
    k=k_ref[...].astype(F32); v=v_ref[...].astype(F32)
    tail=jnp.where(at<3,-1.0,0.0).astype(F32)
    zero=jnp.zeros_like(k)
    kx=(jnp.where(left,k,tail).astype(BF),jnp.where(left,tail,k).astype(BF))
    km=(jnp.where(left,k,zero).astype(BF),jnp.where(left,zero,k).astype(BF))
    vx=(jnp.where(left,v,tail).astype(BF),jnp.where(left,tail,v).astype(BF))
    for i in range(length//bq):
        at_q=pl.ds(i*bq,bq)
        q=q_ref[at_q,:].astype(F32)*0.125
        l=l_ref[at_q,:].astype(F32)
        g=g_ref[at_q,:].astype(F32)
        zq=jnp.zeros_like(q)
        prod=g*o_ref[at_q,:].astype(F32)
        da=jnp.sum(jnp.where(leftq,prod,zq),axis=1,keepdims=True)
        db=jnp.sum(jnp.where(leftq,zq,prod),axis=1,keepdims=True)
        d=spread(jnp.where(leftq,db,da),lq).astype(F32)
        qx=(jnp.where(leftq,q,l).astype(BF),jnp.where(leftq,l,q).astype(BF))
        qm=(jnp.where(leftq,q,zq).astype(BF),jnp.where(leftq,zq,q).astype(BF))
        gx=(jnp.where(leftq,g,d).astype(BF),jnp.where(leftq,d,g).astype(BF))
        gm=(jnp.where(leftq,g,zq).astype(BF),jnp.where(leftq,zq,g).astype(BF))
        gq=None; gk=None; gv=None
        for h in range(2):
            p=jnp.exp(dot(kx[h],qx[h],NT))
            ds=(p*dot(vx[h],gx[h],NT)).astype(BF)
            tv=dot(p.astype(BF),gm[h],NN); tk=dot(ds,qm[h],NN); tq=dot(ds,km[h],TN)
            gq=tq if gq is None else gq+tq
            gk=tk if gk is None else gk+tk
            gv=tv if gv is None else gv+tv
        out_ref[at_q,cols[0]]=(gq*0.125).astype(BF)
        if i==0: ak[...]=gk; av[...]=gv
        else: ak[...]+=gk; av[...]+=gv
    out_ref[:,cols[1]]=ak[...].astype(BF)
    out_ref[:,cols[2]]=av[...].astype(BF)


def attn_bwd(qkv, mixed, lse, gmixed, first, rows, bq=256):
    n = qkv.shape[0]
    length = n // rows
    width = qkv.shape[1] // 3
    pairs = width // 128

    def spec(off):
        return pl.BlockSpec((length, 128), lambda s, p: (s, off + p))

    return pl.pallas_call(
        functools.partial(bwd_kernel, bq),
        grid=(rows, pairs),
        in_specs=[
            spec(0),
            spec(pairs),
            spec(2 * pairs),
            spec(0),
            spec(0),
            spec(first),
        ],
        out_specs=pl.BlockSpec((length, 3 * width), lambda s, p: (s, 0)),
        out_shape=jax.ShapeDtypeStruct((n, 3 * width), BF),
        scratch_shapes=[pltpu.VMEM((length, 128), F32)] * 2,
        compiler_params=pltpu.CompilerParams(vmem_limit_bytes=56 << 20),
        cost_estimate=pl.CostEstimate(
            flops=52 * n * length * width,
            bytes_accessed=n * width * 18,
            transcendentals=n * length * width // 64,
        ),
        name="attention_backward",
    )(qkv, qkv, qkv, mixed, lse, gmixed)


def mid_kernel(T, at, x_any, m0_any, m1_any, g, mine, other, back_mine, back_other, vec_ref, fb_ref,
               out_ref, gh_ref, gm_ref, keep, send, sum_ref, fs_ref,
               wo, wi_s, wb_s, gi_s, gb_s, n2, n2t, gt, xh, acc, ai, ab, sem, wsem, gsem):
    f, nf = pl.program_id(0), pl.num_programs(0)
    core = at[0]
    n, D = n2.shape
    F = wi_s.shape[2]
    blocks, half, r = n // T, D // 2, D // 8
    x_ref, m_ref, gtw = out_ref, gm_ref, gh_ref

    def weights(step, slot):
        part, local = step // (nf // 2), lax.rem(step, nf // 2)
        cols = pl.ds(pl.multiple_of(half + local * F, 128), F)
        rows = pl.ds(pl.multiple_of(step * F, 128), F)
        left = pl.ds(pl.multiple_of(core * half, 128), half)
        right = pl.ds(pl.multiple_of((1 - core) * half, 128), half)
        return part, (
            pltpu.make_async_copy(mine.at[:, cols], wi_s.at[slot], wsem.at[slot, 0]),
            pltpu.make_async_copy(other.at[:, cols], wi_s.at[slot], wsem.at[slot, 0]),
            pltpu.make_async_copy(back_mine.at[rows, :], wb_s.at[slot, :, left], wsem.at[slot, 1]),
            pltpu.make_async_copy(back_other.at[rows, :], wb_s.at[slot, :, right], wsem.at[slot, 2]),
        )

    def fetch(step, slot):
        part, (a, b, c, d) = weights(step, slot)

        @pl.when(part == core)
        def _():
            a.start()

        @pl.when(part != core)
        def _():
            b.start()

        c.start()
        d.start()

    def grads(step):
        part, local = step // (nf // 2), lax.rem(step, nf // 2)
        out = []
        per = F // half
        for w in range(8):
            for k in range(per):
                row = pl.multiple_of(r + (local * per + k) * r, r)
                out.append((part, w, pl.ds(row, r), gi_s.at[w * r : (w + 1) * r, k * half : (k + 1) * half]))
        for k in range(per):
            for h in range(2):
                out.append((h, step * per + k, pl.ds(5 * r, half), gb_s.at[h * half : (h + 1) * half, k * half : (k + 1) * half]))
        return out

    def store(copies, first):
        for i, (part, w, rows, src) in enumerate(copies):
            @pl.when(part == core)
            def _():
                pltpu.make_async_copy(src, keep.at[w, rows, :], gsem.at[first + i]).start()

            @pl.when(part != core)
            def _():
                pltpu.make_async_copy(src, send.at[w, rows, :], gsem.at[first + i]).start()

    def settle(copies, first):
        for i, (part, w, rows, src) in enumerate(copies):
            pltpu.make_async_copy(src, keep.at[w, rows, :], gsem.at[first + i]).wait()

    slot = lax.rem(f, 2)

    @pl.when(f == 0)
    def _():
        cx = pltpu.make_async_copy(x_any, x_ref, sem.at[0])
        cx.start()
        start = 0
        cm = []
        for j, a in enumerate((m0_any, m1_any)):
            w = a.shape[1]
            cm.append(pltpu.make_async_copy(a, m_ref.at[:, pl.ds(start, w)], sem.at[1 + j]))
            start += w
        left = pl.ds(pl.multiple_of(core * half, 128), half)
        right = pl.ds(pl.multiple_of((1 - core) * half, 128), half)
        cm.append(pltpu.make_async_copy(mine.at[:, pl.ds(0, half)], wo.at[:, left], sem.at[3]))
        cm.append(pltpu.make_async_copy(other.at[:, pl.ds(0, half)], wo.at[:, right], sem.at[4]))
        for copy in cm:
            copy.start()
        fetch(0, 0)
        for copy in [cx] + cm:
            copy.wait()

        @pl.loop(0, blocks)
        def _(i):
            at_t = pl.ds(pl.multiple_of(i * T, T), T)
            hidden = x_ref[at_t, :].astype(F32) + dot(m_ref[at_t, :], wo[...], NN) + vec_ref[2:3, :]
            c = hidden - jnp.mean(hidden, axis=1, keepdims=True)
            inv = lax.rsqrt(jnp.mean(c * c, axis=1, keepdims=True) + EPS)
            nn = (c * inv * vec_ref[0:1, :] + vec_ref[1:2, :]).astype(BF)
            acc[at_t, :] = hidden + vec_ref[3:4, :]
            xh[at_t, :] = c
            n2[at_t, :] = nn
            n2t[:, at_t] = nn.T
            gt[:, at_t] = g[at_t, :].T

    @pl.when(f < nf - 1)
    def _():
        fetch(f + 1, 1 - slot)

    _, (a, b, c, d) = weights(f, slot)
    a.wait()
    c.wait()
    d.wait()
    wi_ref, wb_ref = wi_s.at[slot], wb_s.at[slot]
    fs = None
    for i in range(blocks):
        at_t = pl.ds(i * T, T)
        pre = dot(n2[at_t, :], wi_ref[...], NN) + fb_ref[...]
        ga = dot(g[at_t, :], wb_ref[...], NT)
        sq = pre * pre
        t = jnp.tanh(pre * (ROOT + (ROOT * CUBIC) * sq))
        part = 0.5 * pre
        act = (part + part * t).astype(BF)
        slope = (0.5 + 0.5 * t) + part * (1.0 - t * t) * (ROOT + (3 * ROOT * CUBIC) * sq)
        gp = (ga * slope).astype(BF)
        s = jnp.sum(gp.astype(F32), axis=0, keepdims=True)
        fs = s if fs is None else fs + s
        a = dot(n2t[:, i * T : (i + 1) * T], gp, NN)
        b = dot(gt[:, i * T : (i + 1) * T], act, NN)
        if i == 0:
            ai[...] = a
            ab[...] = b
        elif i < blocks - 1:
            ai[...] += a
            ab[...] += b
        else:
            @pl.when(f > 0)
            def _():
                settle(grads(f - 1), 0)

            gi_s[...] = (ai[...] + a).astype(BF)
            gb_s[...] = (ab[...] + b).astype(BF)
            store(grads(f), 0)
        acc[at_t, :] += dot(act, wb_ref[...], NN)
        gtwo = dot(gp, wi_ref[...], NT)

        @pl.when(f == 0)
        def _():
            gtw[at_t, :] = gtwo

        @pl.when(f > 0)
        def _():
            gtw[at_t, :] += gtwo

    fs_ref[...] = fs

    @pl.when(f == nf - 1)
    def _():
        sum_ref[...] = jnp.zeros_like(sum_ref)
        ai[...] = jnp.zeros_like(ai)

        @pl.loop(0, blocks)
        def _(i):
            at_t = pl.ds(pl.multiple_of(i * T, T), T)
            out_ref[at_t, :] = acc[at_t, :].astype(BF)
            gtwo, c = gtw[at_t, :], xh[at_t, :]
            inv = lax.rsqrt(jnp.mean(c * c, axis=1, keepdims=True) + EPS)
            xhat = c * inv
            e = gtwo * vec_ref[0:1, :]
            m1 = jnp.mean(e, axis=1, keepdims=True)
            m2 = jnp.mean(e * xhat, axis=1, keepdims=True)
            gg = g[at_t, :].astype(F32)
            gh = gg + inv * (e - m1 - xhat * m2)
            gh_ref[at_t, :] = gh
            ga = gh.astype(BF)
            ai[...] += dot(m_ref[at_t, :], ga, TN)
            gm_ref[at_t, :] = dot(ga, wo[...], NT).astype(BF)
            rows = (gtwo * xhat, gtwo, ga.astype(F32), gg)
            sum_ref[...] += jnp.concatenate([jnp.sum(v, axis=0, keepdims=True) for v in rows], axis=0)

        settle(grads(f), 0)
        gi_s[...] = ai[...].astype(BF)
        last_ones = [
            (h, w, pl.ds(0, r), gi_s.at[w * r : (w + 1) * r, h * half : (h + 1) * half])
            for w in range(8)
            for h in range(2)
        ]
        store(last_ones, 0)
        settle(last_ones, 0)


def middle(core, x, mixed, g, mine, other, back_mine, back_other, vec, fb, F=768, T=256):
    n, D = x.shape
    FF = fb.shape[1]
    one = pl.Buffered(1)

    def full(shape):
        return pl.BlockSpec(shape, lambda f: (0, 0), pipeline_mode=one)

    anywhere = pl.BlockSpec(memory_space=pl.ANY)
    packed = (8, D // 8 + 2 * FF // 16 + D // 2, D // 2)
    return pl.pallas_call(
        functools.partial(mid_kernel, T),
        grid=(FF // F,),
        in_specs=[pl.BlockSpec(memory_space=pltpu.SMEM)]
        + [anywhere] * 3
        + [full((n, D))]
        + [anywhere] * 4
        + [full((4, D)), pl.BlockSpec((1, F), lambda f: (0, f))],
        out_specs=[full((n, D)), full((n, D)), full((n, D)), anywhere, anywhere]
        + [full((4, D)), pl.BlockSpec((1, F), lambda f: (0, f))],
        out_shape=[
            jax.ShapeDtypeStruct((n, D), BF),
            jax.ShapeDtypeStruct((n, D), F32),
            jax.ShapeDtypeStruct((n, D), BF),
            jax.ShapeDtypeStruct(packed, BF),
            jax.ShapeDtypeStruct(packed, BF),
            jax.ShapeDtypeStruct((4, D), F32),
            jax.ShapeDtypeStruct((1, FF), F32),
        ],
        scratch_shapes=[
            pltpu.VMEM((D, D), BF),
            pltpu.VMEM((2, D, F), BF),
            pltpu.VMEM((2, F, D), BF),
            pltpu.VMEM((D, F), BF),
            pltpu.VMEM((D, F), BF),
            pltpu.VMEM((n, D), BF),
            pltpu.VMEM((D, n), BF),
            pltpu.VMEM((D, n), BF),
            pltpu.VMEM((n, D), F32),
            pltpu.VMEM((n, D), F32),
            pltpu.VMEM((D, F), F32),
            pltpu.VMEM((D, F), F32),
            pltpu.SemaphoreType.DMA((5,)),
            pltpu.SemaphoreType.DMA((2, 3)),
            pltpu.SemaphoreType.DMA((20,)),
        ],
        compiler_params=pltpu.CompilerParams(vmem_limit_bytes=63 << 20),
        cost_estimate=pl.CostEstimate(
            flops=24 * n * D * FF,
            bytes_accessed=n * D * 16 + 12 * D * FF,
            transcendentals=n * FF,
        ),
        name="feed_forward",
    )(core, x, *mixed, g, mine, other, back_mine, back_other, vec, fb)


def last_kernel(x_ref, gh_ref, gain_ref, *refs):
    groups = (len(refs) - 2) // 2
    grads, weights = refs[:groups], refs[groups : 2 * groups]
    out_ref, sum_ref = refs[2 * groups :]
    x = x_ref[...].astype(F32)
    c = x - jnp.mean(x, axis=1, keepdims=True)
    inv = lax.rsqrt(jnp.mean(c * c, axis=1, keepdims=True) + EPS)
    xhat = c * inv
    one = None
    for grad, weight in zip(grads, weights):
        part = dot(grad[...], weight[...], NT)
        one = part if one is None else one + part
    e = one * gain_ref[...]
    m1 = jnp.mean(e, axis=1, keepdims=True)
    m2 = jnp.mean(e * xhat, axis=1, keepdims=True)
    out_ref[...] = gh_ref[...] + inv * (e - m1 - xhat * m2)
    sums = [one * xhat, one] + [grad[...].astype(F32) for grad in grads]
    sums = jnp.concatenate([jnp.sum(v, axis=0, keepdims=True) for v in sums], axis=1)

    @pl.when(pl.program_id(0) == 0)
    def _():
        sum_ref[...] = sums

    @pl.when(pl.program_id(0) > 0)
    def _():
        sum_ref[...] += sums


def last(x, gh, gain, grads, weights, T=256):
    n, D = x.shape
    total = 2 * D + sum(grad.shape[1] for grad in grads)
    block = pl.BlockSpec((T, D), lambda i: (i, 0))
    return pl.pallas_call(
        last_kernel,
        grid=(n // T,),
        in_specs=[block, block, pl.BlockSpec((1, D), lambda i: (0, 0))]
        + [pl.BlockSpec((T, grad.shape[1]), lambda i: (i, 0)) for grad in grads]
        + [pl.BlockSpec(weight.shape, lambda i: (0, 0)) for weight in weights],
        out_specs=[block, pl.BlockSpec((1, total), lambda i: (0, 0))],
        out_shape=[jax.ShapeDtypeStruct((n, D), F32), jax.ShapeDtypeStruct((1, total), F32)],
        compiler_params=pltpu.CompilerParams(vmem_limit_bytes=56 << 20),
        cost_estimate=pl.CostEstimate(
            flops=12 * n * D * D, bytes_accessed=n * D * 16, transcendentals=0
        ),
        name="input_gradient",
    )(x, gh, gain, *grads, *weights)


def project_kernel(order, rows, half, at, n1, mine, other, bias, qkv, w, sem):
    me, core = at[0], at[1]

    @pl.when(pl.program_id(0) == 0)
    def _():
        copies = []
        for i, o in enumerate(order):
            row = pl.ds(pl.multiple_of((me ^ o) * rows, rows), rows)
            for src, part in ((mine, core), (other, 1 - core)):
                col = pl.ds(pl.multiple_of(part * half, 128), half)
                copies.append(
                    pltpu.make_async_copy(src.at[i, pl.ds(0, rows), :], w.at[row, col], sem.at[len(copies)])
                )
        for copy in copies:
            copy.start()
        for copy in copies:
            copy.wait()

    qkv[...] = (dot(n1[...], w[...], NN) + bias[...]).astype(BF)


def project(n1, mine, other, order, rows, bias, T=512):
    n, D = n1.shape
    half = mine.shape[2]
    me, core = lax.axis_index("wide"), lax.axis_index("narrow") & 1
    if rows % 16:
        mine, other = [natural(p[:, :rows], order).reshape(-1, half) for p in (mine, other)]
        w = jnp.where(core == 0, jnp.concatenate([mine, other], 1), jnp.concatenate([other, mine], 1))
        return (dot(n1, w, NN) + bias).astype(BF), w
    anywhere = pl.BlockSpec(memory_space=pl.ANY)
    return pl.pallas_call(
        functools.partial(project_kernel, order, rows, half),
        grid=(n // T,),
        in_specs=[
            pl.BlockSpec(memory_space=pltpu.SMEM),
            pl.BlockSpec((T, D), lambda i: (i, 0)),
            anywhere,
            anywhere,
            pl.BlockSpec((1, 2 * half), lambda i: (0, 0)),
        ],
        out_specs=[
            pl.BlockSpec((T, 2 * half), lambda i: (i, 0)),
            pl.BlockSpec((D, 2 * half), lambda i: (0, 0)),
        ],
        out_shape=[
            jax.ShapeDtypeStruct((n, 2 * half), BF),
            jax.ShapeDtypeStruct((D, 2 * half), BF),
        ],
        scratch_shapes=[pltpu.SemaphoreType.DMA((2 * len(order),))],
        compiler_params=pltpu.CompilerParams(vmem_limit_bytes=56 << 20),
        cost_estimate=pl.CostEstimate(
            flops=8 * n * D * half, bytes_accessed=n * D * 4 + n * half * 4, transcendentals=0
        ),
        name="project",
    )(jnp.stack([me, core]).astype(jnp.int32), n1, mine, other, bias)


def swap(x, axis, mask):
    size = lax.axis_size(axis)
    return lax.ppermute(x, axis, [(i, i ^ mask) for i in range(size)])


def bit_groups(size):
    top = size.bit_length() - 1
    cuts = [(0, 1)]
    low = 1
    while low < top:
        high = min(low + 2, top)
        cuts.append((low, high))
        low = high
    return cuts


def gather_wide(piece):
    size = lax.axis_size("wide")
    me = lax.axis_index("wide")
    stack, order = piece[None], [0]
    for low, high in reversed(bit_groups(size)):
        masks = [m << low for m in range(1 << (high - low))]
        stack = jnp.concatenate([stack] + [swap(stack, "wide", m) for m in masks[1:]])
        order = [o ^ m for m in masks for o in order]
    return stack, order


def natural(stack, order):
    size = len(order)
    me = lax.axis_index("wide")
    place = jnp.argsort(jnp.array(order))
    return jnp.take(stack, place[me ^ jnp.arange(size)], axis=0)


def gather(piece):
    mine, order = gather_wide(piece)
    return mine, swap(mine, "narrow", 1), order


def half_of(x, index, size, axis):
    return lax.dynamic_slice_in_dim(x, index * size, size, axis)


def add(*terms):
    total = terms[0].astype(F32)
    for term in terms[1:]:
        total = total + term.astype(F32)
    return total.astype(BF)


def scatter_wide(x):
    me = lax.axis_index("wide")
    size = x.shape[0]
    for low, high in bit_groups(size):
        ways = 1 << (high - low)
        mine = (me >> low) & (ways - 1)
        split = x.reshape((x.shape[0] // ways, ways) + x.shape[1:])
        got = [lax.dynamic_index_in_dim(split, mine, 1, keepdims=False)]
        for m in range(1, ways):
            sent = lax.dynamic_index_in_dim(split, mine ^ m, 1, keepdims=False)
            got.append(swap(sent, "wide", m << low))
        x = add(*got)
    return x[0]


def exchange(mine):
    core = lax.axis_index("narrow") & 1
    mine = add(mine, swap(mine, "narrow", 2))
    other = swap(mine, "narrow", 1)
    return [jnp.where(core == 0, mine, other), jnp.where(core == 0, other, mine)]


def reduce(grad):
    half = grad.shape[2] // 2
    core = lax.axis_index("narrow") & 1
    kept = add(half_of(grad, core, half, 2), swap(half_of(grad, 1 - core, half, 2), "narrow", 1))
    return jnp.concatenate(exchange(scatter_wide(kept)), axis=1).astype(F32)


def reduce_small(x):
    me = lax.axis_index("wide")
    for low, high in bit_groups(x.shape[0]):
        ways = 1 << (high - low)
        mine = (me >> low) & (ways - 1)
        split = x.reshape((x.shape[0] // ways, ways) + x.shape[1:])
        got = [lax.dynamic_index_in_dim(split, mine, 1, keepdims=False)]
        for m in range(1, ways):
            got.append(swap(lax.dynamic_index_in_dim(split, mine ^ m, 1, keepdims=False), "wide", m << low))
        x = sum(got[1:], got[0])
    x = x[0]
    a, b, c = [swap(x, "narrow", m) for m in (1, 2, 3)]
    return (x + a) + (b + c)


def regroup(summed, size):
    eight, depth, step = summed.shape
    r = 2 * step // eight
    rows = summed[:, : 5 * r].reshape(eight, 5, r, step).transpose(0, 2, 1, 3).reshape(size, -1, 5, step)
    rows = rows.transpose(0, 2, 1, 3).reshape(size, -1, step)
    back = summed[:, 5 * r :].transpose(1, 0, 2).reshape(step, size, -1).transpose(1, 0, 2)
    return jnp.concatenate([rows, back.reshape(size, -1, step)], axis=1).reshape(-1, step)


def body(tokens, cotangent, row_kind, grad_mask, w_qkv, w_out, w_in, w_back, norm_gain, norm_shift, proj_bias, ffn_bias):
    rows, length, width = tokens.shape
    n = rows * length
    size = lax.axis_size("wide")
    share = width // size
    core = lax.axis_index("narrow") & 1
    packed = jnp.concatenate([norm_gain, norm_shift, proj_bias, ffn_bias.reshape(-1, share)])
    cuts = [0, width // 3, width]
    split = w_qkv.reshape(share, 3, width)
    pieces = []
    for low, high in zip(cuts, cuts[1:]):
        columns = split[:, :, low:high].reshape(share, 3 * (high - low))
        pieces.append(half_of(columns, core, 3 * (high - low) // 2, 1))
    half = pieces[0].shape[1]
    extra = jnp.pad(packed.reshape(-1), (0, 16 * half - packed.size)).reshape(16, half)
    pieces[0] = jnp.concatenate([pieces[0], extra])
    gathered = [gather(piece) for piece in pieces]
    small = natural(gathered[0][0][:, share:], gathered[0][2])
    small = small.reshape(size, -1)[:, : packed.size].reshape((size,) + packed.shape).astype(F32)
    hid = w_in.shape[1] // 2
    piece = jnp.concatenate(
        [half_of(w_out, core, width // 2, 1), half_of(w_in, core, hid, 1)]
        + [half_of(w_back[i * share : (i + 1) * share], core, width // 2, 1) for i in range(w_back.shape[0] // share)],
        axis=1,
    )
    mine = lax.all_gather(piece, "wide", axis=0, tiled=True)
    other = swap(mine, "narrow", 1)

    def back_half(gathered):
        chunks = gathered[:, width // 2 + hid :].reshape(size, share, -1, width // 2)
        return chunks.transpose(0, 2, 1, 3).reshape(-1, width // 2)

    by_column = small[:, :8].transpose(1, 0, 2).reshape(8, width)
    gains, shifts, biases = by_column[:2], by_column[2:4], by_column[4:8]
    ffn_bias_full = small[:, 8:].reshape(1, -1)
    x = tokens.reshape(n, width)
    inputs = x.astype(F32)
    centred = inputs - jnp.mean(inputs, axis=-1, keepdims=True)
    inv = lax.rsqrt(jnp.mean(centred * centred, axis=-1, keepdims=True) + EPS)
    normed_one = (centred * inv * gains[0] + shifts[0]).astype(BF)
    keep = jnp.where(row_kind[:, None] == 1, jnp.ones(grad_mask.shape, F32), grad_mask.astype(F32))
    g_ffn = (cotangent.astype(F32) * keep[:, :, None]).reshape(n, width).astype(BF)
    qkv, mixed, lse, w_groups = [], [], [], []
    for g, (low, high) in enumerate(zip(cuts, cuts[1:])):
        bias = jnp.concatenate([biases[0, low:high], jnp.zeros((high - low,), F32), biases[1, low:high]])
        got, w = project(normed_one, *gathered[g], share, bias[None])
        qkv.append(got)
        w_groups.append(w)
        m, l = attn_fwd(got, rows)
        mixed.append(m)
        lse.append(l)
    vec = jnp.stack([gains[1], shifts[1], biases[2], biases[3]])
    layer_out, g_hidden, g_mixed, kept, sent, sums, ffn_sum = middle(
        core[None], x, mixed, g_ffn, mine, other, back_half(mine), back_half(other), vec, ffn_bias_full
    )
    summed = add(kept, swap(sent, "narrow", 1))
    if size != summed.shape[0]:
        summed = regroup(summed, size)
    else:
        summed = summed.reshape(-1, summed.shape[2])
    summed = lax.psum_scatter(summed, "wide", scatter_dimension=0, tiled=True)
    left, right = exchange(summed)
    step = width // 2
    both = [t.astype(F32) for t in (left, right)]
    share_out = jnp.concatenate([t[:share] for t in both], axis=1)
    share_in = jnp.concatenate(
        [t[i * share : (i + 1) * share] for t in both for i in range(1, 5)], axis=1
    )
    share_back = jnp.concatenate([t[5 * share :].reshape(step, -1) for t in both], axis=0).T
    g_groups, share_groups = [None, None], [None, None]
    for g in (1, 0):
        low, high = cuts[g], cuts[g + 1]
        g_groups[g] = attn_bwd(qkv[g], mixed[g], lse[g], g_mixed, low // 128, rows)
        grad = dot(normed_one, g_groups[g], TN).astype(BF)
        share_groups[g] = reduce(grad.reshape(size, share, -1)).reshape(share, 3, high - low)
    input_grad, last_sums = last(x, g_hidden, gains[:1], g_groups, w_groups)
    last_sums = last_sums[0]
    columns, at = [], 2 * width
    for low, high in zip(cuts, cuts[1:]):
        columns.append(last_sums[at : at + 3 * (high - low)].reshape(3, high - low))
        at += 3 * (high - low)
    column_sums = jnp.concatenate(columns, axis=1)
    by_column = jnp.stack(
        [last_sums[:width], sums[0], last_sums[width : 2 * width], sums[1], column_sums[0], column_sums[2], sums[2], sums[3]]
    )
    by_column = by_column.reshape(8, size, share).transpose(1, 0, 2)
    small = reduce_small(jnp.concatenate([by_column, ffn_sum.reshape(size, -1, share)], axis=1))
    return (
        layer_out.reshape(rows, length, width),
        input_grad.reshape(rows, length, width),
        jnp.concatenate(share_groups, axis=2).reshape(share, 3 * width),
        share_out,
        share_in,
        share_back,
        small[:2],
        small[2:4],
        small[4:8],
        small[8:].reshape(-1),
    )


def solution(mesh):
    in_specs = (
        P(("wide", "narrow"), None, None),
        P(("wide", "narrow"), None, None),
        P(("wide", "narrow")),
        P(("wide", "narrow"), None),
        P("wide", None),
        P("wide", None),
        P("wide", None),
        P("wide", None),
        P(None, "wide"),
        P(None, "wide"),
        P(None, "wide"),
        P("wide"),
    )
    out_specs = (
        P(("wide", "narrow"), None, None),
        P(("wide", "narrow"), None, None),
        P("wide", None),
        P("wide", None),
        P("wide", None),
        P("wide", None),
        P(None, "wide"),
        P(None, "wide"),
        P(None, "wide"),
        P("wide"),
    )
    return jax.shard_map(body, mesh=mesh, in_specs=in_specs, out_specs=out_specs, check_vma=False)
```

```python
import functools

import jax
import jax.numpy as jnp
from jax import lax
from jax.experimental import pallas as pl
from jax.experimental.pallas import tpu as pltpu
from jax.sharding import PartitionSpec as P

HEADS = 12
F32 = jnp.float32
BF = jnp.bfloat16
EPS = 1e-05
ROOT = 0.7978845608028654
CUBIC = 0.044715
NN = (((1,), (0,)), ((), ()))
NT = (((1,), (1,)), ((), ()))
TN = (((0,), (0,)), ((), ()))


def dot(a, b, dims):
    return lax.dot_general(a, b, dims, preferred_element_type=F32)


def spread(x, lane):
    hi = x.astype(BF).astype(F32)
    rest = x - hi
    mid = rest.astype(BF).astype(F32)
    at = lane & 63
    zero = jnp.zeros_like(x)
    picked = jnp.where(at == 0, hi, jnp.where(at == 1, mid, jnp.where(at == 2, rest - mid, zero)))
    return picked.astype(BF)

def fwd_kernel(bq, x_ref, o_ref, l_ref, *_):
    length = x_ref.shape[0]
    lane = lax.broadcasted_iota(jnp.int32, (length, 128), 1)
    left = lane < 64
    lq = lax.broadcasted_iota(jnp.int32, (bq, 128), 1)
    leftq = lq < 64
    k = x_ref[:, 128:256]
    v = x_ref[:, 256:384].astype(F32)
    ones = jnp.ones_like(v)
    va = jnp.where(left, v, ones).astype(BF)
    vb = jnp.where(left, ones, v).astype(BF)
    for i in range(length // bq):
        q = x_ref[i * bq : (i + 1) * bq, :128].astype(F32) * 0.125
        zero = jnp.zeros_like(q)
        qa = jnp.where(leftq, q, zero).astype(BF)
        qb = jnp.where(leftq, zero, q).astype(BF)
        outs, peaks = [], []
        for qq, vv in ((qa, va), (qb, vb)):
            s = dot(qq, k, NT)
            m = jnp.max(s, axis=1, keepdims=True)
            p = jnp.exp(s - m).astype(BF)
            outs.append(dot(p, vv, NN))
            peaks.append(m)
        oa, ob = outs
        num = jnp.where(leftq, oa, ob)
        den = jnp.where(leftq, ob, oa)
        o_ref[i * bq : (i + 1) * bq, :] = (num / pltpu.roll(den, 64, 1)).astype(BF)
        lse = jnp.where(leftq, peaks[1], peaks[0]) + jnp.log(den)
        l_ref[i * bq : (i + 1) * bq, :] = spread(lse, lq)


def attn_fwd(qkv, first, pairs, rows, deps=(), bq=512):
    n = qkv.shape[0]
    length = n // rows
    width = pairs * 128
    out = pl.BlockSpec((length, 128), lambda s, p: (s, p))

    def kernel(x_ref, *refs):
        fwd_kernel(bq, x_ref, *refs[len(deps) :])

    return pl.pallas_call(
        kernel,
        grid=(rows, pairs),
        in_specs=[pl.BlockSpec((length, 384), lambda s, p: (s, first + p))]
        + [pl.BlockSpec(memory_space=pl.ANY)] * len(deps),
        out_specs=[out, out],
        out_shape=[jax.ShapeDtypeStruct((n, width), BF)] * 2,
        compiler_params=pltpu.CompilerParams(vmem_limit_bytes=56 << 20),
        cost_estimate=pl.CostEstimate(
            flops=30 * n * length * width,
            bytes_accessed=n * width * 10,
            transcendentals=n * length * width // 64,
        ),
        name="attention_forward",
    )(qkv, *deps)


def bwd_kernel(bq, at, x_ref, o_ref, l_ref, g_ref, n1t_ref, out_ref, keep_ref, send_ref, sum_ref, ak, av, dw):
    length = x_ref.shape[0]
    p, s, last = pl.program_id(0), pl.program_id(1), pl.num_programs(1) - 1
    lane = lax.broadcasted_iota(jnp.int32, (length, 128), 1)
    left = lane < 64
    lq = lax.broadcasted_iota(jnp.int32, (bq, 128), 1)
    leftq = lq < 64
    k = x_ref[:, 128:256].astype(F32)
    v = x_ref[:, 256:384].astype(F32)
    tail = jnp.where((lane & 63) < 3, -1.0, 0.0).astype(F32)
    zero = jnp.zeros_like(k)
    kx = (jnp.where(left, k, tail).astype(BF), jnp.where(left, tail, k).astype(BF))
    km = (jnp.where(left, k, zero).astype(BF), jnp.where(left, zero, k).astype(BF))
    vx = (jnp.where(left, v, tail).astype(BF), jnp.where(left, tail, v).astype(BF))
    for i in range(length // bq):
        here = slice(i * bq, (i + 1) * bq)
        q = x_ref[here, :128].astype(F32) * 0.125
        l = l_ref[here, :].astype(F32)
        g = g_ref[here, :].astype(F32)
        zq = jnp.zeros_like(q)
        prod = g * o_ref[here, :].astype(F32)
        da = jnp.sum(jnp.where(leftq, prod, zq), axis=1, keepdims=True)
        db = jnp.sum(jnp.where(leftq, zq, prod), axis=1, keepdims=True)
        d = spread(jnp.where(leftq, db, da), lq).astype(F32)
        qx = (jnp.where(leftq, q, l).astype(BF), jnp.where(leftq, l, q).astype(BF))
        qm = (jnp.where(leftq, q, zq).astype(BF), jnp.where(leftq, zq, q).astype(BF))
        gx = (jnp.where(leftq, g, d).astype(BF), jnp.where(leftq, d, g).astype(BF))
        gm = (jnp.where(leftq, g, zq).astype(BF), jnp.where(leftq, zq, g).astype(BF))
        gq = gk = gv = None
        for h in range(2):
            pr = jnp.exp(dot(kx[h], qx[h], NT))
            ds = (pr * dot(vx[h], gx[h], NT)).astype(BF)
            tv = dot(pr.astype(BF), gm[h], NN)
            tk = dot(ds, qm[h], NN)
            tq = dot(ds, km[h], TN)
            gq = tq if gq is None else gq + tq
            gk = tk if gk is None else gk + tk
            gv = tv if gv is None else gv + tv
        out_ref[here, :128] = (gq * 0.125).astype(BF)
        if i == 0:
            ak[...] = gk
            av[...] = gv
        else:
            ak[...] += gk
            av[...] += gv
    out_ref[:, 128:256] = ak[...].astype(BF)
    out_ref[:, 256:384] = av[...].astype(BF)
    got = out_ref[...]
    grad = dot(n1t_ref[...], got, NN)
    sums = jnp.sum(got.astype(F32), axis=0, keepdims=True)

    @pl.when(s == 0)
    def _():
        dw[...] = grad
        sum_ref[...] = jnp.broadcast_to(sums, (8, 384))

    @pl.when((s > 0) & (s < last))
    def _():
        dw[...] += grad

    @pl.when(s > 0)
    def _():
        sum_ref[...] += jnp.broadcast_to(sums, (8, 384))

    @pl.when((s == last) & (p == at[0]))
    def _():
        keep_ref[...] = (dw[...] + grad).astype(BF)

    @pl.when((s == last) & (p != at[0]))
    def _():
        send_ref[...] = (dw[...] + grad).astype(BF)


def attn_bwd(core, qkv, first, mixed, lse, gmixed, at_g, n1t, rows, deps=(), bq=256):
    n = qkv.shape[0]
    length = n // rows
    D = n1t.shape[0]
    pairs = 2
    block = pl.BlockSpec((length, 128), lambda p, s: (s, p))
    whole = pl.BlockSpec((D, 384), lambda p, s: (0, 0))

    def kernel(at, x, o, l, g, t, *refs):
        bwd_kernel(bq, at, x, o, l, g, t, *refs[len(deps) :])

    assert rows > 1
    return pl.pallas_call(
        kernel,
        grid=(pairs, rows),
        in_specs=[
            pl.BlockSpec(memory_space=pltpu.SMEM),
            pl.BlockSpec((length, 384), lambda p, s: (s, first + p)),
            block,
            block,
            pl.BlockSpec((length, 128), lambda p, s: (s, at_g + p)),
            pl.BlockSpec((D, length), lambda p, s: (0, s)),
        ]
        + [pl.BlockSpec(memory_space=pl.ANY)] * len(deps),
        out_specs=[
            pl.BlockSpec((length, 384), lambda p, s: (s, p)),
            whole,
            whole,
            pl.BlockSpec((8, 384), lambda p, s: (0, p)),
        ],
        out_shape=[
            jax.ShapeDtypeStruct((n, pairs * 384), BF),
            jax.ShapeDtypeStruct((D, 384), BF),
            jax.ShapeDtypeStruct((D, 384), BF),
            jax.ShapeDtypeStruct((8, pairs * 384), F32),
        ],
        scratch_shapes=[pltpu.VMEM((length, 128), F32)] * 2 + [pltpu.VMEM((D, 384), F32)],
        compiler_params=pltpu.CompilerParams(vmem_limit_bytes=56 << 20),
        cost_estimate=pl.CostEstimate(
            flops=56 * n * length * pairs * 128,
            bytes_accessed=n * pairs * 128 * 18,
            transcendentals=n * length * pairs * 2,
        ),
        name="attention_backward",
    )(core, qkv, mixed, lse, gmixed, n1t, *deps)


def tie_kernel(a, b, out):
    pass


def tie(x, after):
    anywhere = pl.BlockSpec(memory_space=pl.ANY)
    return pl.pallas_call(
        tie_kernel,
        in_specs=[anywhere] * 2,
        out_specs=anywhere,
        out_shape=jax.ShapeDtypeStruct(x.shape, x.dtype),
        input_output_aliases={0: 0},
        name="tie",
    )(x, after)


def mid_kernel(T, direct, at, x_any, m0_any, m1_any, m2_any, g, mine, other, back_mine, back_other, vec_ref, fb_ref,
               out_ref, gh_ref, gm_ref, keep, send, keep_b, send_b, sum_ref, fs_ref,
               wo, wi_s, wb_s, gi_s, gb_s, n2, n2t, gt, xh, acc, ai, ab, sem, wsem, gsem):
    f, nf = pl.program_id(0), pl.num_programs(0)
    core = at[0]
    n, D = n2.shape
    F = wi_s.shape[2]
    blocks, half, r = n // T, D // 2, D // 8
    at_back = mine.shape[1] - (half // r) * half
    x_ref, m_ref, gtw = out_ref, gm_ref, gh_ref

    left = pl.ds(pl.multiple_of(core * half, 128), half)
    right = pl.ds(pl.multiple_of((1 - core) * half, 128), half)

    def back(step, slot):
        if not direct:
            rows = pl.ds(pl.multiple_of(step * F, 128), F)
            return [(back_mine.at[rows, :], wb_s.at[slot, :, left]), (back_other.at[rows, :], wb_s.at[slot, :, right])]
        out = []
        for k in range(F // half):
            rows = pl.ds(pl.multiple_of((step * (F // half) + k) * r, r), r)
            for t in range(half // r):
                cols = pl.ds(at_back + t * half, half)
                to = slice(k * half + t * r, k * half + (t + 1) * r)
                out.append((mine.at[rows, cols], wb_s.at[slot, to, left]))
                out.append((other.at[rows, cols], wb_s.at[slot, to, right]))
        return out

    def inner(step):
        return pl.ds(pl.multiple_of(half + lax.rem(step, nf // 2) * F, 128), F)

    def fetch(step, slot):
        @pl.when(step // (nf // 2) == core)
        def _():
            pltpu.make_async_copy(mine.at[:, inner(step)], wi_s.at[slot], wsem.at[slot, 0]).start()

        @pl.when(step // (nf // 2) != core)
        def _():
            pltpu.make_async_copy(other.at[:, inner(step)], wi_s.at[slot], wsem.at[slot, 0]).start()

        for i, (src, to) in enumerate(back(step, slot)):
            pltpu.make_async_copy(src, to, wsem.at[slot, 1 + i]).start()

    def grads(step):
        part, local = step // (nf // 2), lax.rem(step, nf // 2)
        out = []
        per = F // half
        for w in range(8):
            for k in range(per):
                row = pl.multiple_of(r + (local * per + k) * r, r)
                src = gi_s.at[w * r : (w + 1) * r, k * half : (k + 1) * half]
                out.append((part, (keep, send), w, pl.ds(row, r), src))
        for k in range(per):
            for h in range(2):
                src = gb_s.at[h * half : (h + 1) * half, k * half : (k + 1) * half]
                out.append((h, (keep_b, send_b), step * per + k, pl.ds(0, half), src))
        return out

    def store(copies):
        for i, (part, to, w, rows, src) in enumerate(copies):
            @pl.when(part == core)
            def _():
                pltpu.make_async_copy(src, to[0].at[w, rows, :], gsem.at[i]).start()

            @pl.when(part != core)
            def _():
                pltpu.make_async_copy(src, to[1].at[w, rows, :], gsem.at[i]).start()

    def settle(copies):
        for i, (part, to, w, rows, src) in enumerate(copies):
            pltpu.make_async_copy(src, to[0].at[w, rows, :], gsem.at[i]).wait()

    slot = lax.rem(f, 2)

    @pl.when(f == 0)
    def _():
        cx = pltpu.make_async_copy(x_any, x_ref, sem.at[0])
        cx.start()
        start = 0
        cm = []
        for j, a in enumerate((m0_any, m1_any, m2_any)):
            w = a.shape[1]
            cm.append(pltpu.make_async_copy(a, m_ref.at[:, pl.ds(start, w)], sem.at[1 + j]))
            start += w
        cm.append(pltpu.make_async_copy(mine.at[:, pl.ds(0, half)], wo.at[:, left], sem.at[4]))
        cm.append(pltpu.make_async_copy(other.at[:, pl.ds(0, half)], wo.at[:, right], sem.at[5]))
        for copy in cm:
            copy.start()
        fetch(0, 0)
        for copy in [cx] + cm:
            copy.wait()

        @pl.loop(0, blocks)
        def _(i):
            at_t = pl.ds(pl.multiple_of(i * T, T), T)
            hidden = x_ref[at_t, :].astype(F32) + dot(m_ref[at_t, :], wo[...], NN) + vec_ref[2:3, :]
            c = hidden - jnp.mean(hidden, axis=1, keepdims=True)
            inv = lax.rsqrt(jnp.mean(c * c, axis=1, keepdims=True) + EPS)
            nn = (c * inv * vec_ref[0:1, :] + vec_ref[1:2, :]).astype(BF)
            acc[at_t, :] = hidden + vec_ref[3:4, :]
            xh[at_t, :] = c
            n2[at_t, :] = nn
            n2t[:, at_t] = nn.T
            gt[:, at_t] = g[at_t, :].T

    @pl.when(f < nf - 1)
    def _():
        fetch(f + 1, 1 - slot)

    pltpu.make_async_copy(mine.at[:, inner(f)], wi_s.at[slot], wsem.at[slot, 0]).wait()
    for i, (src, to) in enumerate(back(f, slot)):
        pltpu.make_async_copy(src, to, wsem.at[slot, 1 + i]).wait()
    wi_ref, wb_ref = wi_s.at[slot], wb_s.at[slot]
    fs = None
    for i in range(blocks):
        at_t = pl.ds(i * T, T)
        pre = dot(n2[at_t, :], wi_ref[...], NN) + fb_ref[...]
        ga = dot(g[at_t, :], wb_ref[...], NT)
        sq = pre * pre
        t = jnp.tanh(pre * (ROOT + (ROOT * CUBIC) * sq))
        part = 0.5 * pre
        act = (part + part * t).astype(BF)
        slope = (0.5 + 0.5 * t) + part * (1.0 - t * t) * (ROOT + (3 * ROOT * CUBIC) * sq)
        gp = (ga * slope).astype(BF)
        s = jnp.sum(gp.astype(F32), axis=0, keepdims=True)
        fs = s if fs is None else fs + s
        a = dot(n2t[:, i * T : (i + 1) * T], gp, NN)
        b = dot(gt[:, i * T : (i + 1) * T], act, NN)
        if i == 0:
            ai[...] = a
            ab[...] = b
        elif i < blocks - 1:
            ai[...] += a
            ab[...] += b
        else:
            @pl.when(f > 0)
            def _():
                settle(grads(f - 1))

            gi_s[...] = (ai[...] + a).astype(BF)
            gb_s[...] = (ab[...] + b).astype(BF)
            store(grads(f))
        acc[at_t, :] += dot(act, wb_ref[...], NN)
        gtwo = dot(gp, wi_ref[...], NT)

        @pl.when(f == 0)
        def _():
            gtw[at_t, :] = gtwo

        @pl.when(f > 0)
        def _():
            gtw[at_t, :] += gtwo

    fs_ref[...] = fs

    @pl.when(f == nf - 1)
    def _():
        sum_ref[...] = jnp.zeros_like(sum_ref)
        ai[...] = jnp.zeros_like(ai)

        @pl.loop(0, blocks)
        def _(i):
            at_t = pl.ds(pl.multiple_of(i * T, T), T)
            out_ref[at_t, :] = acc[at_t, :].astype(BF)
            gtwo, c = gtw[at_t, :], xh[at_t, :]
            inv = lax.rsqrt(jnp.mean(c * c, axis=1, keepdims=True) + EPS)
            xhat = c * inv
            e = gtwo * vec_ref[0:1, :]
            m1 = jnp.mean(e, axis=1, keepdims=True)
            m2 = jnp.mean(e * xhat, axis=1, keepdims=True)
            gg = g[at_t, :].astype(F32)
            gh = gg + inv * (e - m1 - xhat * m2)
            gh_ref[at_t, :] = gh
            ga = gh.astype(BF)
            ai[...] += dot(m_ref[at_t, :], ga, TN)
            gm_ref[at_t, :] = dot(ga, wo[...], NT).astype(BF)
            rows = (gtwo * xhat, gtwo, ga.astype(F32), gg)
            sum_ref[...] += jnp.concatenate([jnp.sum(v, axis=0, keepdims=True) for v in rows], axis=0)

        settle(grads(f))
        gi_s[...] = ai[...].astype(BF)
        last_ones = [
            (h, (keep, send), w, pl.ds(0, r), gi_s.at[w * r : (w + 1) * r, h * half : (h + 1) * half])
            for w in range(8)
            for h in range(2)
        ]
        store(last_ones)
        settle(last_ones)


def middle(core, x, mixed, g, mine, other, back_mine, back_other, direct, vec, fb, F=768, T=256):
    n, D = x.shape
    FF = fb.shape[1]
    one = pl.Buffered(1)

    def full(shape):
        return pl.BlockSpec(shape, lambda f: (0, 0), pipeline_mode=one)

    anywhere = pl.BlockSpec(memory_space=pl.ANY)
    packed = (8, D // 8 + FF // 8, D // 2)
    packed_b = (8, D // 2, FF // 8)
    return pl.pallas_call(
        functools.partial(mid_kernel, T, direct),
        grid=(FF // F,),
        in_specs=[pl.BlockSpec(memory_space=pltpu.SMEM)]
        + [anywhere] * 4
        + [full((n, D))]
        + [anywhere] * 4
        + [full((4, D)), pl.BlockSpec((1, F), lambda f: (0, f))],
        out_specs=[full((n, D)), full((n, D)), full((n, D))] + [anywhere] * 4
        + [full((4, D)), pl.BlockSpec((1, F), lambda f: (0, f))],
        out_shape=[
            jax.ShapeDtypeStruct((n, D), BF),
            jax.ShapeDtypeStruct((n, D), F32),
            jax.ShapeDtypeStruct((n, D), BF),
            jax.ShapeDtypeStruct(packed, BF),
            jax.ShapeDtypeStruct(packed, BF),
            jax.ShapeDtypeStruct(packed_b, BF),
            jax.ShapeDtypeStruct(packed_b, BF),
            jax.ShapeDtypeStruct((4, D), F32),
            jax.ShapeDtypeStruct((1, FF), F32),
        ],
        scratch_shapes=[
            pltpu.VMEM((D, D), BF),
            pltpu.VMEM((2, D, F), BF),
            pltpu.VMEM((2, F, D), BF),
            pltpu.VMEM((D, F), BF),
            pltpu.VMEM((D, F), BF),
            pltpu.VMEM((n, D), BF),
            pltpu.VMEM((D, n), BF),
            pltpu.VMEM((D, n), BF),
            pltpu.VMEM((n, D), F32),
            pltpu.VMEM((n, D), F32),
            pltpu.VMEM((D, F), F32),
            pltpu.VMEM((D, F), F32),
            pltpu.SemaphoreType.DMA((6,)),
            pltpu.SemaphoreType.DMA((2, 17)),
            pltpu.SemaphoreType.DMA((20,)),
        ],
        compiler_params=pltpu.CompilerParams(vmem_limit_bytes=63 << 20),
        cost_estimate=pl.CostEstimate(
            flops=24 * n * D * FF,
            bytes_accessed=n * D * 16 + 12 * D * FF,
            transcendentals=n * FF,
        ),
        name="feed_forward",
    )(core, x, *mixed, g, mine, other, back_mine, back_other, vec, fb)


def last_kernel(x_ref, gh_ref, gain_ref, *refs):
    grads, w0, w1 = refs[:3], refs[3], refs[4]
    out_ref, sum_ref = refs[-2:]
    x = x_ref[...].astype(F32)
    c = x - jnp.mean(x, axis=1, keepdims=True)
    inv = lax.rsqrt(jnp.mean(c * c, axis=1, keepdims=True) + EPS)
    xhat = c * inv
    half = w1.shape[1] // 2
    one = dot(grads[0][...], w0[...], NT)
    one += dot(grads[1][...], w1[:, :half], NT)
    one += dot(grads[2][...], w1[:, half:], NT)
    e = one * gain_ref[...]
    m1 = jnp.mean(e, axis=1, keepdims=True)
    m2 = jnp.mean(e * xhat, axis=1, keepdims=True)
    out_ref[...] = gh_ref[...] + inv * (e - m1 - xhat * m2)
    sums = jnp.concatenate([jnp.sum(v, axis=0, keepdims=True) for v in (one * xhat, one)], axis=0)

    @pl.when(pl.program_id(0) == 0)
    def _():
        sum_ref[...] = sums

    @pl.when(pl.program_id(0) > 0)
    def _():
        sum_ref[...] += sums


def last(x, gh, gain, grads, weights, deps=(), T=512):
    n, D = x.shape
    block = pl.BlockSpec((T, D), lambda i: (i, 0))
    return pl.pallas_call(
        last_kernel,
        grid=(n // T,),
        in_specs=[block, block, pl.BlockSpec((1, D), lambda i: (0, 0))]
        + [block] * 3
        + [pl.BlockSpec(weight.shape, lambda i: (0, 0)) for weight in weights]
        + [pl.BlockSpec(memory_space=pl.ANY)] * len(deps),
        out_specs=[block, pl.BlockSpec((2, D), lambda i: (0, 0))],
        out_shape=[jax.ShapeDtypeStruct((n, D), F32), jax.ShapeDtypeStruct((2, D), F32)],
        compiler_params=pltpu.CompilerParams(vmem_limit_bytes=56 << 20),
        cost_estimate=pl.CostEstimate(
            flops=12 * n * D * D, bytes_accessed=n * D * 16, transcendentals=0
        ),
        name="input_gradient",
    )(x, gh, gain, *grads, *weights, *deps)


def project_kernel(order, rows, half, at, n1, mine, other, bias, *refs):
    qkv, w, sem = refs[-3:]
    me, core = at[0], at[1]

    @pl.when(pl.program_id(0) == 0)
    def _():
        copies = []
        for i, o in enumerate(order):
            row = pl.ds(pl.multiple_of((me ^ o) * rows, rows), rows)
            for src, part in ((mine, core), (other, 1 - core)):
                col = pl.ds(pl.multiple_of(part * half, 128), half)
                copies.append(
                    pltpu.make_async_copy(src.at[i, pl.ds(0, rows), :], w.at[row, col], sem.at[len(copies)])
                )
        for copy in copies:
            copy.start()
        for copy in copies:
            copy.wait()

    qkv[...] = (dot(n1[...], w[...], NN) + bias[...]).astype(BF)


def project(n1, mine, other, order, rows, bias, deps=(), T=512):
    n, D = n1.shape
    half = mine.shape[2]
    me, core = lax.axis_index("wide"), lax.axis_index("narrow") & 1
    if rows % 16:
        mine, other = [natural(p[:, :rows], order).reshape(-1, half) for p in (mine, other)]
        w = jnp.where(core == 0, jnp.concatenate([mine, other], 1), jnp.concatenate([other, mine], 1))
        return (dot(n1, w, NN) + bias).astype(BF), w
    anywhere = pl.BlockSpec(memory_space=pl.ANY)
    return pl.pallas_call(
        functools.partial(project_kernel, order, rows, half),
        grid=(n // T,),
        in_specs=[
            pl.BlockSpec(memory_space=pltpu.SMEM),
            pl.BlockSpec((T, D), lambda i: (i, 0)),
            anywhere,
            anywhere,
            pl.BlockSpec((1, 2 * half), lambda i: (0, 0)),
        ]
        + [anywhere] * len(deps),
        out_specs=[
            pl.BlockSpec((T, 2 * half), lambda i: (i, 0)),
            pl.BlockSpec((D, 2 * half), lambda i: (0, 0)),
        ],
        out_shape=[
            jax.ShapeDtypeStruct((n, 2 * half), BF),
            jax.ShapeDtypeStruct((D, 2 * half), BF),
        ],
        scratch_shapes=[pltpu.SemaphoreType.DMA((2 * len(order),))],
        compiler_params=pltpu.CompilerParams(vmem_limit_bytes=56 << 20),
        cost_estimate=pl.CostEstimate(
            flops=8 * n * D * half, bytes_accessed=n * D * 4 + n * half * 4, transcendentals=0
        ),
        name="project",
    )(jnp.stack([me, core]).astype(jnp.int32), n1, mine, other, bias, *deps)


def swap(x, axis, mask):
    size = lax.axis_size(axis)
    return lax.ppermute(x, axis, [(i, i ^ mask) for i in range(size)])


def bit_groups(size):
    top = size.bit_length() - 1
    cuts = [(0, 1)]
    low = 1
    while low < top:
        high = min(low + 2, top)
        cuts.append((low, high))
        low = high
    return cuts


def gather_wide(piece):
    size = lax.axis_size("wide")
    me = lax.axis_index("wide")
    stack, order = piece[None], [0]
    for low, high in reversed(bit_groups(size)):
        masks = [m << low for m in range(1 << (high - low))]
        stack = jnp.concatenate([stack] + [swap(stack, "wide", m) for m in masks[1:]])
        order = [o ^ m for m in masks for o in order]
    return stack, order


def natural(stack, order):
    size = len(order)
    me = lax.axis_index("wide")
    place = jnp.argsort(jnp.array(order))
    return jnp.take(stack, place[me ^ jnp.arange(size)], axis=0)


def gather(piece):
    mine, order = gather_wide(piece)
    return mine, swap(mine, "narrow", 1), order


def half_of(x, index, size, axis):
    return lax.dynamic_slice_in_dim(x, index * size, size, axis)


def add(*terms):
    total = terms[0].astype(F32)
    for term in terms[1:]:
        total = total + term.astype(F32)
    return total.astype(BF)


def scatter_wide(x):
    me = lax.axis_index("wide")
    size = x.shape[0]
    for low, high in bit_groups(size):
        ways = 1 << (high - low)
        mine = (me >> low) & (ways - 1)
        split = x.reshape((x.shape[0] // ways, ways) + x.shape[1:])
        got = [lax.dynamic_index_in_dim(split, mine, 1, keepdims=False)]
        for m in range(1, ways):
            sent = lax.dynamic_index_in_dim(split, mine ^ m, 1, keepdims=False)
            got.append(swap(sent, "wide", m << low))
        x = add(*got)
    return x[0]


def pick(x, low, high):
    me = lax.axis_index("wide")
    ways = 1 << (high - low)
    mine = (me >> low) & (ways - 1)
    split = [t.reshape((t.shape[0] // ways, ways) + t.shape[1:]) for t in x]
    return [add(*[lax.dynamic_index_in_dim(t, mine ^ m, 1, keepdims=False) for t in split]) for m in range(ways)]


def send(picked, low):
    return [picked[0]] + [swap(t, "wide", m << low) for m, t in enumerate(picked) if m]


def regroup(blocks, size):
    eight, depth, step = blocks.shape
    r = depth // 5
    blocks = blocks.reshape(eight, 5, r, step).transpose(0, 2, 1, 3).reshape(size, -1, 5, step)
    return blocks.transpose(0, 2, 1, 3).reshape(size, -1, step)


def regroup_back(blocks, size):
    eight, depth, step = blocks.shape
    blocks = blocks.transpose(1, 0, 2).reshape(depth, size, -1)
    return blocks.transpose(1, 0, 2)


def body(tokens, cotangent, row_kind, grad_mask, w_qkv, w_out, w_in, w_back, norm_gain, norm_shift, proj_bias, ffn_bias):
    rows, length, width = tokens.shape
    n = rows * length
    size = lax.axis_size("wide")
    share = width // size
    core = lax.axis_index("narrow") & 1
    packed = jnp.concatenate([norm_gain, norm_shift, proj_bias, ffn_bias.reshape(-1, share)])
    pairs = width // 128
    by_pair = w_qkv.reshape(share, 3, pairs, 128).transpose(0, 2, 1, 3).reshape(share, 3 * width)
    pieces = [half_of(by_pair[:, :768], core, 384, 1), half_of(by_pair[:, 768:], core, 768, 1)]
    extra = jnp.pad(packed.reshape(-1), (0, 16 * 384 - packed.size)).reshape(16, 384)
    pieces[0] = jnp.concatenate([pieces[0], extra])
    gathered = [gather(piece) for piece in pieces]
    small = natural(gathered[0][0][:, share:], gathered[0][2])
    small = small.reshape(size, -1)[:, : packed.size].reshape((size,) + packed.shape).astype(F32)
    hid = w_in.shape[1] // 2
    piece = jnp.concatenate(
        [half_of(w_out, core, width // 2, 1), half_of(w_in, core, hid, 1)]
        + [half_of(w_back[i * share : (i + 1) * share], core, width // 2, 1) for i in range(w_back.shape[0] // share)],
        axis=1,
    )
    mine = lax.all_gather(piece, "wide", axis=0, tiled=True)

    def back_half(gathered):
        chunks = gathered[:, width // 2 + hid :].reshape(size, share, -1, width // 2)
        return chunks.transpose(0, 2, 1, 3).reshape(-1, width // 2)

    by_column = small[:, :8].transpose(1, 0, 2).reshape(8, width)
    gains, shifts, biases = by_column[:2], by_column[2:4], by_column[4:8]
    ffn_bias_full = small[:, 8:].reshape(1, -1)
    x = tokens.reshape(n, width)
    inputs = x.astype(F32)
    centred = inputs - jnp.mean(inputs, axis=-1, keepdims=True)
    inv = lax.rsqrt(jnp.mean(centred * centred, axis=-1, keepdims=True) + EPS)
    normed_one = (centred * inv * gains[0] + shifts[0]).astype(BF)
    keep = jnp.where(row_kind[:, None] == 1, jnp.ones(grad_mask.shape, F32), grad_mask.astype(F32))
    g_ffn = (cotangent.astype(F32) * keep[:, :, None]).reshape(n, width).astype(BF)
    n1t = normed_one.T
    bias = jnp.stack([biases[0], jnp.zeros((width,), F32), biases[1]])
    bias = bias.reshape(3, pairs, 128).transpose(1, 0, 2).reshape(1, -1)
    qkv_a, w_a = project(normed_one, *gathered[0], share, bias[:, :768])
    mixed_a, lse_a = attn_fwd(qkv_a, 0, 2, rows)
    qkv_b, w_b = project(normed_one, *gathered[1], share, bias[:, 768:], deps=(mixed_a,))
    mixed_b, lse_b = attn_fwd(qkv_b, 0, 2, rows)
    mine = tie(mine, mixed_b)
    other = swap(mine, "narrow", 1)
    mixed_c, lse_c = attn_fwd(qkv_b, 2, 2, rows, deps=(mine,))
    vec = jnp.stack([gains[1], shifts[1], biases[2], biases[3]])
    direct = size == 8 and share % 16 == 0
    backs = (mine, other) if direct else (back_half(mine), back_half(other))
    at = core[None]
    layer_out, g_hidden, g_mixed, kept, sent, kept_b, sent_b, sums, ffn_sum = middle(
        at, x, (mixed_a, mixed_b, mixed_c), g_ffn, mine, other, *backs, direct, vec, ffn_bias_full
    )
    if size != 8:
        kept, sent, kept_b, sent_b = (
            regroup(kept, size), regroup(sent, size), regroup_back(kept_b, size), regroup_back(sent_b, size)
        )
    groups = [(bit, bit + 1) for bit in range(size.bit_length() - 1)]

    def finish(x, stage):
        for low, high in groups[stage:]:
            x = send(pick(x, low, high), low)
        return add(*x)[0]

    def step_on(x, stage):
        picked = pick(x, *groups[stage])
        return picked, send(picked, groups[stage][0])

    from_core = swap(sent, "narrow", 1)
    from_core_b = swap(sent_b, "narrow", 1)
    g_c, keep_c, send_c, sum_c = attn_bwd(at, qkv_b, 2, mixed_c, lse_c, g_mixed, 4, n1t, rows)
    both = add(kept, from_core)
    picked_b, x_b = step_on([kept_b, from_core_b], 0)
    summed = lax.psum_scatter(both.reshape(-1, both.shape[2]), "wide", scatter_dimension=0, tiled=True)
    from_core_c = swap(send_c, "narrow", 1)
    g_b, keep_d, send_d, sum_b = attn_bwd(
        at, qkv_b, 0, mixed_b, lse_b, g_mixed, 2, n1t, rows, deps=[both, keep_c] + picked_b
    )
    from_core_d = swap(send_d, "narrow", 1)
    picked_b, x_b = step_on(x_b, 1)
    tied = tie(from_core_c, keep_d)
    picked_c, x_c = step_on([t.reshape(size, share, -1) for t in (keep_c, tied)], 0)
    g_a, keep_e, send_e, sum_a = attn_bwd(
        at, qkv_a, 0, mixed_a, lse_a, g_mixed, 0, n1t, rows, deps=picked_b + picked_c + [keep_d]
    )
    from_core_e = swap(send_e, "narrow", 1)
    picked_b, x_b = step_on([x_b[0], tie(x_b[1], keep_e)], 2)
    picked_c, x_c = step_on([x_c[0], tie(x_c[1], keep_e)], 1)
    input_grad, last_sums = last(
        x, g_hidden, gains[:1], (g_a, g_b, g_c), (w_a, w_b), deps=picked_b + picked_c + [from_core_d]
    )
    column_sums = jnp.concatenate([t[0] for t in (sum_a, sum_b, sum_c)])
    column_sums = column_sums.reshape(pairs, 3, 128).transpose(1, 0, 2).reshape(3, width)
    by_column = jnp.stack(
        [last_sums[0], sums[0], last_sums[1], sums[1], column_sums[0], column_sums[2], sums[2], sums[3]]
    )
    by_column = by_column.reshape(8, size, share).transpose(1, 0, 2)
    small = jnp.concatenate([by_column, ffn_sum.reshape(size, -1, share)], axis=1).astype(BF).reshape(size, -1)
    count = small.shape[1]
    extra = -(-count // 768)
    small = jnp.pad(small, ((0, 0), (0, extra * 768 - count))).reshape(size, extra, 768)
    halves = [pick([t.reshape(size, share, -1) for t in ts], *groups[0]) for ts in ((keep_d, from_core_d), (keep_e, from_core_e))]
    picked = [
        jnp.concatenate([jnp.concatenate([d, e], axis=2), s], axis=1)
        for d, e, s in zip(*halves, pick([small], *groups[0]))
    ]
    x_b = [x_b[0], tie(x_b[1], last_sums)]
    x_c = [x_c[0], tie(x_c[1], last_sums)]
    block_b = finish(x_b, 3)
    early = jnp.concatenate([summed, block_b.reshape(-1, width // 2)], axis=0)
    early_y = swap(early, "narrow", 2)
    x_de = send(picked, 0)
    picked_c, x_c = step_on(x_c, 2)
    early = add(early, early_y)
    early_core = swap(early, "narrow", 1)
    x_de = [x_de[0], tie(x_de[1], early)]
    _, x_de = step_on(x_de, 1)
    x_de = [x_de[0], tie(x_de[1], early_core)]
    late = finish(x_de, 2)
    more = finish(x_c, 3)
    late = jnp.concatenate([late, jnp.pad(more, ((0, extra), (0, 0)))], axis=1)
    late = add(late, swap(late, "narrow", 2))
    late_core = swap(late, "narrow", 1)

    def ordered(mine, other):
        return [jnp.where(core == 0, mine, other), jnp.where(core == 0, other, mine)]

    left, right = ordered(early, early_core)
    five, step = 5 * share, width // 2
    share_out = jnp.concatenate([t[:share] for t in (left, right)], axis=1).astype(F32)
    share_in = jnp.concatenate(
        [t[i * share : (i + 1) * share] for t in (left, right) for i in range(1, 5)], axis=1
    ).astype(F32)
    share_back = jnp.concatenate([t[five:].reshape(step, -1).T for t in (left, right)], axis=1).astype(F32)
    small = late[share:, :768].astype(F32) + late_core[share:, :768].astype(F32)
    small = small.reshape(-1)[:count].reshape(-1, share)
    left, right = ordered(late[:share], late_core[:share])
    share_qkv = jnp.stack([left[:, 384:768], right[:, 384:768], left[:, :384], right[:, :384], left[:, 768:], right[:, 768:]], axis=1)
    share_qkv = share_qkv.reshape(share, pairs, 3, 128).transpose(0, 2, 1, 3).reshape(share, -1).astype(F32)
    return (
        layer_out.reshape(rows, length, width),
        input_grad.reshape(rows, length, width),
        share_qkv,
        share_out,
        share_in,
        share_back,
        small[:2],
        small[2:4],
        small[4:8],
        small[8:].reshape(-1),
    )


def solution(mesh):
    in_specs = (
        P(("wide", "narrow"), None, None),
        P(("wide", "narrow"), None, None),
        P(("wide", "narrow")),
        P(("wide", "narrow"), None),
        P("wide", None),
        P("wide", None),
        P("wide", None),
        P("wide", None),
        P(None, "wide"),
        P(None, "wide"),
        P(None, "wide"),
        P("wide"),
    )
    out_specs = (
        P(("wide", "narrow"), None, None),
        P(("wide", "narrow"), None, None),
        P("wide", None),
        P("wide", None),
        P("wide", None),
        P("wide", None),
        P(None, "wide"),
        P(None, "wide"),
        P(None, "wide"),
        P("wide"),
    )
    return jax.shard_map(body, mesh=mesh, in_specs=in_specs, out_specs=out_specs, check_vma=False)
```

```python
import functools

import jax
import jax.numpy as jnp
from jax import lax
from jax.experimental import pallas as pl
from jax.experimental.pallas import tpu as pltpu
from jax.sharding import PartitionSpec as P

HEADS = 12
F32 = jnp.float32
BF = jnp.bfloat16
EPS = 1e-05
ROOT = 0.7978845608028654
CUBIC = 0.044715
NN = (((1,), (0,)), ((), ()))
NT = (((1,), (1,)), ((), ()))
TN = (((0,), (0,)), ((), ()))


def dot(a, b, dims):
    return lax.dot_general(a, b, dims, preferred_element_type=F32)


def spread(x, lane):
    hi = x.astype(BF).astype(F32)
    rest = x - hi
    mid = rest.astype(BF).astype(F32)
    at = lane & 63
    zero = jnp.zeros_like(x)
    picked = jnp.where(at == 0, hi, jnp.where(at == 1, mid, jnp.where(at == 2, rest - mid, zero)))
    return picked.astype(BF)

def fwd_kernel(bq, x_ref, o_ref, l_ref, *_):
    length = x_ref.shape[0]
    lane = lax.broadcasted_iota(jnp.int32, (length, 128), 1)
    left = lane < 64
    lq = lax.broadcasted_iota(jnp.int32, (bq, 128), 1)
    leftq = lq < 64
    k = x_ref[:, 128:256]
    v = x_ref[:, 256:384].astype(F32)
    ones = jnp.ones_like(v)
    va = jnp.where(left, v, ones).astype(BF)
    vb = jnp.where(left, ones, v).astype(BF)
    for i in range(length // bq):
        q = x_ref[i * bq : (i + 1) * bq, :128].astype(F32) * 0.125
        zero = jnp.zeros_like(q)
        qa = jnp.where(leftq, q, zero).astype(BF)
        qb = jnp.where(leftq, zero, q).astype(BF)
        outs, peaks = [], []
        for qq, vv in ((qa, va), (qb, vb)):
            s = dot(qq, k, NT)
            m = jnp.max(s, axis=1, keepdims=True)
            p = jnp.exp(s - m).astype(BF)
            outs.append(dot(p, vv, NN))
            peaks.append(m)
        oa, ob = outs
        num = jnp.where(leftq, oa, ob)
        den = jnp.where(leftq, ob, oa)
        o_ref[i * bq : (i + 1) * bq, :] = (num / pltpu.roll(den, 64, 1)).astype(BF)
        lse = jnp.where(leftq, peaks[1], peaks[0]) + jnp.log(den)
        l_ref[i * bq : (i + 1) * bq, :] = spread(lse, lq)


def attn_fwd(qkv, first, pairs, rows, deps=(), bq=512):
    n = qkv.shape[0]
    length = n // rows
    width = pairs * 128
    out = pl.BlockSpec((length, 128), lambda s, p: (s, p))

    def kernel(x_ref, *refs):
        fwd_kernel(bq, x_ref, *refs[len(deps) :])

    return pl.pallas_call(
        kernel,
        grid=(rows, pairs),
        in_specs=[pl.BlockSpec((length, 384), lambda s, p: (s, first + p))]
        + [pl.BlockSpec(memory_space=pl.ANY)] * len(deps),
        out_specs=[out, out],
        out_shape=[jax.ShapeDtypeStruct((n, width), BF)] * 2,
        compiler_params=pltpu.CompilerParams(vmem_limit_bytes=56 << 20),
        cost_estimate=pl.CostEstimate(
            flops=30 * n * length * width,
            bytes_accessed=n * width * 10,
            transcendentals=n * length * width // 64,
        ),
        name="attention_forward",
    )(qkv, *deps)


def bwd_kernel(bq, at, x_ref, o_ref, l_ref, g_ref, n1t_ref, out_ref, keep_ref, send_ref, sum_ref, ak, av, dw):
    length = x_ref.shape[0]
    p, s, last = pl.program_id(0), pl.program_id(1), pl.num_programs(1) - 1
    lane = lax.broadcasted_iota(jnp.int32, (length, 128), 1)
    left = lane < 64
    lq = lax.broadcasted_iota(jnp.int32, (bq, 128), 1)
    leftq = lq < 64
    k = x_ref[:, 128:256].astype(F32)
    v = x_ref[:, 256:384].astype(F32)
    tail = jnp.where((lane & 63) < 3, -1.0, 0.0).astype(F32)
    zero = jnp.zeros_like(k)
    kx = (jnp.where(left, k, tail).astype(BF), jnp.where(left, tail, k).astype(BF))
    km = (jnp.where(left, k, zero).astype(BF), jnp.where(left, zero, k).astype(BF))
    vx = (jnp.where(left, v, tail).astype(BF), jnp.where(left, tail, v).astype(BF))
    for i in range(length // bq):
        here = slice(i * bq, (i + 1) * bq)
        q = x_ref[here, :128].astype(F32) * 0.125
        l = l_ref[here, :].astype(F32)
        g = g_ref[here, :].astype(F32)
        zq = jnp.zeros_like(q)
        prod = g * o_ref[here, :].astype(F32)
        da = jnp.sum(jnp.where(leftq, prod, zq), axis=1, keepdims=True)
        db = jnp.sum(jnp.where(leftq, zq, prod), axis=1, keepdims=True)
        d = spread(jnp.where(leftq, db, da), lq).astype(F32)
        qx = (jnp.where(leftq, q, l).astype(BF), jnp.where(leftq, l, q).astype(BF))
        qm = (jnp.where(leftq, q, zq).astype(BF), jnp.where(leftq, zq, q).astype(BF))
        gx = (jnp.where(leftq, g, d).astype(BF), jnp.where(leftq, d, g).astype(BF))
        gm = (jnp.where(leftq, g, zq).astype(BF), jnp.where(leftq, zq, g).astype(BF))
        gq = gk = gv = None
        for h in range(2):
            pr = jnp.exp(dot(kx[h], qx[h], NT))
            ds = (pr * dot(vx[h], gx[h], NT)).astype(BF)
            tv = dot(pr.astype(BF), gm[h], NN)
            tk = dot(ds, qm[h], NN)
            tq = dot(ds, km[h], TN)
            gq = tq if gq is None else gq + tq
            gk = tk if gk is None else gk + tk
            gv = tv if gv is None else gv + tv
        out_ref[here, :128] = (gq * 0.125).astype(BF)
        if i == 0:
            ak[...] = gk
            av[...] = gv
        else:
            ak[...] += gk
            av[...] += gv
    out_ref[:, 128:256] = ak[...].astype(BF)
    out_ref[:, 256:384] = av[...].astype(BF)
    got = out_ref[...]
    grad = dot(n1t_ref[...], got, NN)
    sums = jnp.sum(got.astype(F32), axis=0, keepdims=True)

    @pl.when(s == 0)
    def _():
        dw[...] = grad
        sum_ref[...] = jnp.broadcast_to(sums, (8, 384))

    @pl.when((s > 0) & (s < last))
    def _():
        dw[...] += grad

    @pl.when(s > 0)
    def _():
        sum_ref[...] += jnp.broadcast_to(sums, (8, 384))

    @pl.when((s == last) & (p == at[0]))
    def _():
        keep_ref[...] = (dw[...] + grad).astype(BF)

    @pl.when((s == last) & (p != at[0]))
    def _():
        send_ref[...] = (dw[...] + grad).astype(BF)


def attn_bwd(core, qkv, first, mixed, lse, gmixed, at_g, n1t, rows, deps=(), bq=256):
    n = qkv.shape[0]
    length = n // rows
    D = n1t.shape[0]
    pairs = 2
    block = pl.BlockSpec((length, 128), lambda p, s: (s, p))
    whole = pl.BlockSpec((D, 384), lambda p, s: (0, 0))

    def kernel(at, x, o, l, g, t, *refs):
        bwd_kernel(bq, at, x, o, l, g, t, *refs[len(deps) :])

    assert rows > 1
    return pl.pallas_call(
        kernel,
        grid=(pairs, rows),
        in_specs=[
            pl.BlockSpec(memory_space=pltpu.SMEM),
            pl.BlockSpec((length, 384), lambda p, s: (s, first + p)),
            block,
            block,
            pl.BlockSpec((length, 128), lambda p, s: (s, at_g + p)),
            pl.BlockSpec((D, length), lambda p, s: (0, s)),
        ]
        + [pl.BlockSpec(memory_space=pl.ANY)] * len(deps),
        out_specs=[
            pl.BlockSpec((length, 384), lambda p, s: (s, p)),
            whole,
            whole,
            pl.BlockSpec((8, 384), lambda p, s: (0, p)),
        ],
        out_shape=[
            jax.ShapeDtypeStruct((n, pairs * 384), BF),
            jax.ShapeDtypeStruct((D, 384), BF),
            jax.ShapeDtypeStruct((D, 384), BF),
            jax.ShapeDtypeStruct((8, pairs * 384), F32),
        ],
        scratch_shapes=[pltpu.VMEM((length, 128), F32)] * 2 + [pltpu.VMEM((D, 384), F32)],
        compiler_params=pltpu.CompilerParams(vmem_limit_bytes=56 << 20),
        cost_estimate=pl.CostEstimate(
            flops=56 * n * length * pairs * 128,
            bytes_accessed=n * pairs * 128 * 18,
            transcendentals=n * length * pairs * 2,
        ),
        name="attention_backward",
    )(core, qkv, mixed, lse, gmixed, n1t, *deps)


def tie_kernel(a, b, out):
    pass


def tie(x, after):
    anywhere = pl.BlockSpec(memory_space=pl.ANY)
    return pl.pallas_call(
        tie_kernel,
        in_specs=[anywhere] * 2,
        out_specs=anywhere,
        out_shape=jax.ShapeDtypeStruct(x.shape, x.dtype),
        input_output_aliases={0: 0},
        name="tie",
    )(x, after)


def mid_kernel(T, direct, at, x_any, m0_any, m1_any, m2_any, g, mine, other, back_mine, back_other, vec_ref, fb_ref,
               out_ref, gh_ref, gm_ref, keep, send, keep_b, send_b, sum_ref, fs_ref,
               wo, wi_s, wb_s, gi_s, gb_s, n2, n2t, gt, xh, acc, ai, ab, sem, wsem, gsem):
    f, nf = pl.program_id(0), pl.num_programs(0)
    core = at[0]
    n, D = n2.shape
    F = wi_s.shape[2]
    blocks, half, r = n // T, D // 2, D // 8
    at_back = mine.shape[1] - (half // r) * half
    x_ref, m_ref, gtw = out_ref, gm_ref, gh_ref

    left = pl.ds(pl.multiple_of(core * half, 128), half)
    right = pl.ds(pl.multiple_of((1 - core) * half, 128), half)

    def back(step, slot):
        if not direct:
            rows = pl.ds(pl.multiple_of(step * F, 128), F)
            return [(back_mine.at[rows, :], wb_s.at[slot, :, left]), (back_other.at[rows, :], wb_s.at[slot, :, right])]
        out = []
        for k in range(F // half):
            rows = pl.ds(pl.multiple_of((step * (F // half) + k) * r, r), r)
            for t in range(half // r):
                cols = pl.ds(at_back + t * half, half)
                to = slice(k * half + t * r, k * half + (t + 1) * r)
                out.append((mine.at[rows, cols], wb_s.at[slot, to, left]))
                out.append((other.at[rows, cols], wb_s.at[slot, to, right]))
        return out

    def inner(step):
        return pl.ds(pl.multiple_of(half + lax.rem(step, nf // 2) * F, 128), F)

    def fetch(step, slot):
        @pl.when(step // (nf // 2) == core)
        def _():
            pltpu.make_async_copy(mine.at[:, inner(step)], wi_s.at[slot], wsem.at[slot, 0]).start()

        @pl.when(step // (nf // 2) != core)
        def _():
            pltpu.make_async_copy(other.at[:, inner(step)], wi_s.at[slot], wsem.at[slot, 0]).start()

        for i, (src, to) in enumerate(back(step, slot)):
            pltpu.make_async_copy(src, to, wsem.at[slot, 1 + i]).start()

    def grads(step):
        part, local = step // (nf // 2), lax.rem(step, nf // 2)
        out = []
        per = F // half
        for w in range(8):
            for k in range(per):
                row = pl.multiple_of(r + (local * per + k) * r, r)
                src = gi_s.at[w * r : (w + 1) * r, k * half : (k + 1) * half]
                out.append((part, (keep, send), w, pl.ds(row, r), src))
        for k in range(per):
            for h in range(2):
                src = gb_s.at[h * half : (h + 1) * half, k * half : (k + 1) * half]
                out.append((h, (keep_b, send_b), step * per + k, pl.ds(0, half), src))
        return out

    def store(copies):
        for i, (part, to, w, rows, src) in enumerate(copies):
            @pl.when(part == core)
            def _():
                pltpu.make_async_copy(src, to[0].at[w, rows, :], gsem.at[i]).start()

            @pl.when(part != core)
            def _():
                pltpu.make_async_copy(src, to[1].at[w, rows, :], gsem.at[i]).start()

    def settle(copies):
        for i, (part, to, w, rows, src) in enumerate(copies):
            pltpu.make_async_copy(src, to[0].at[w, rows, :], gsem.at[i]).wait()

    slot = lax.rem(f, 2)

    @pl.when(f == 0)
    def _():
        cx = pltpu.make_async_copy(x_any, x_ref, sem.at[0])
        cx.start()
        start = 0
        cm = []
        for j, a in enumerate((m0_any, m1_any, m2_any)):
            w = a.shape[1]
            cm.append(pltpu.make_async_copy(a, m_ref.at[:, pl.ds(start, w)], sem.at[1 + j]))
            start += w
        cm.append(pltpu.make_async_copy(mine.at[:, pl.ds(0, half)], wo.at[:, left], sem.at[4]))
        cm.append(pltpu.make_async_copy(other.at[:, pl.ds(0, half)], wo.at[:, right], sem.at[5]))
        for copy in cm:
            copy.start()
        fetch(0, 0)
        for copy in [cx] + cm:
            copy.wait()

        @pl.loop(0, blocks)
        def _(i):
            at_t = pl.ds(pl.multiple_of(i * T, T), T)
            hidden = x_ref[at_t, :].astype(F32) + dot(m_ref[at_t, :], wo[...], NN) + vec_ref[2:3, :]
            c = hidden - jnp.mean(hidden, axis=1, keepdims=True)
            inv = lax.rsqrt(jnp.mean(c * c, axis=1, keepdims=True) + EPS)
            nn = (c * inv * vec_ref[0:1, :] + vec_ref[1:2, :]).astype(BF)
            acc[at_t, :] = hidden + vec_ref[3:4, :]
            xh[at_t, :] = c
            n2[at_t, :] = nn
            n2t[:, at_t] = nn.T
            gt[:, at_t] = g[at_t, :].T

    @pl.when(f < nf - 1)
    def _():
        fetch(f + 1, 1 - slot)

    pltpu.make_async_copy(mine.at[:, inner(f)], wi_s.at[slot], wsem.at[slot, 0]).wait()
    for i, (src, to) in enumerate(back(f, slot)):
        pltpu.make_async_copy(src, to, wsem.at[slot, 1 + i]).wait()
    wi_ref, wb_ref = wi_s.at[slot], wb_s.at[slot]
    fs = None
    for i in range(blocks):
        at_t = pl.ds(i * T, T)
        pre = dot(n2[at_t, :], wi_ref[...], NN) + fb_ref[...]
        ga = dot(g[at_t, :], wb_ref[...], NT)
        sq = pre * pre
        t = jnp.tanh(pre * (ROOT + (ROOT * CUBIC) * sq))
        part = 0.5 * pre
        act = (part + part * t).astype(BF)
        slope = (0.5 + 0.5 * t) + part * (1.0 - t * t) * (ROOT + (3 * ROOT * CUBIC) * sq)
        gp = (ga * slope).astype(BF)
        s = jnp.sum(gp.astype(F32), axis=0, keepdims=True)
        fs = s if fs is None else fs + s
        a = dot(n2t[:, i * T : (i + 1) * T], gp, NN)
        b = dot(gt[:, i * T : (i + 1) * T], act, NN)
        if i == 0:
            ai[...] = a
            ab[...] = b
        elif i < blocks - 1:
            ai[...] += a
            ab[...] += b
        else:
            @pl.when(f > 0)
            def _():
                settle(grads(f - 1))

            gi_s[...] = (ai[...] + a).astype(BF)
            gb_s[...] = (ab[...] + b).astype(BF)
            store(grads(f))
        acc[at_t, :] += dot(act, wb_ref[...], NN)
        gtwo = dot(gp, wi_ref[...], NT)

        @pl.when(f == 0)
        def _():
            gtw[at_t, :] = gtwo

        @pl.when(f > 0)
        def _():
            gtw[at_t, :] += gtwo

    fs_ref[...] = fs

    @pl.when(f == nf - 1)
    def _():
        sum_ref[...] = jnp.zeros_like(sum_ref)
        ai[...] = jnp.zeros_like(ai)

        @pl.loop(0, blocks)
        def _(i):
            at_t = pl.ds(pl.multiple_of(i * T, T), T)
            out_ref[at_t, :] = acc[at_t, :].astype(BF)
            gtwo, c = gtw[at_t, :], xh[at_t, :]
            inv = lax.rsqrt(jnp.mean(c * c, axis=1, keepdims=True) + EPS)
            xhat = c * inv
            e = gtwo * vec_ref[0:1, :]
            m1 = jnp.mean(e, axis=1, keepdims=True)
            m2 = jnp.mean(e * xhat, axis=1, keepdims=True)
            gg = g[at_t, :].astype(F32)
            gh = gg + inv * (e - m1 - xhat * m2)
            gh_ref[at_t, :] = gh
            ga = gh.astype(BF)
            ai[...] += dot(m_ref[at_t, :], ga, TN)
            gm_ref[at_t, :] = dot(ga, wo[...], NT).astype(BF)
            rows = (gtwo * xhat, gtwo, ga.astype(F32), gg)
            sum_ref[...] += jnp.concatenate([jnp.sum(v, axis=0, keepdims=True) for v in rows], axis=0)

        settle(grads(f))
        gi_s[...] = ai[...].astype(BF)
        last_ones = [
            (h, (keep, send), w, pl.ds(0, r), gi_s.at[w * r : (w + 1) * r, h * half : (h + 1) * half])
            for w in range(8)
            for h in range(2)
        ]
        store(last_ones)
        settle(last_ones)


def middle(core, x, mixed, g, mine, other, back_mine, back_other, direct, vec, fb, F=768, T=512):
    n, D = x.shape
    FF = fb.shape[1]
    one = pl.Buffered(1)

    def full(shape):
        return pl.BlockSpec(shape, lambda f: (0, 0), pipeline_mode=one)

    anywhere = pl.BlockSpec(memory_space=pl.ANY)
    packed = (8, D // 8 + FF // 8, D // 2)
    packed_b = (8, D // 2, FF // 8)
    return pl.pallas_call(
        functools.partial(mid_kernel, T, direct),
        grid=(FF // F,),
        in_specs=[pl.BlockSpec(memory_space=pltpu.SMEM)]
        + [anywhere] * 4
        + [full((n, D))]
        + [anywhere] * 4
        + [full((4, D)), pl.BlockSpec((1, F), lambda f: (0, f))],
        out_specs=[full((n, D)), full((n, D)), full((n, D))] + [anywhere] * 4
        + [full((4, D)), pl.BlockSpec((1, F), lambda f: (0, f))],
        out_shape=[
            jax.ShapeDtypeStruct((n, D), BF),
            jax.ShapeDtypeStruct((n, D), F32),
            jax.ShapeDtypeStruct((n, D), BF),
            jax.ShapeDtypeStruct(packed, BF),
            jax.ShapeDtypeStruct(packed, BF),
            jax.ShapeDtypeStruct(packed_b, BF),
            jax.ShapeDtypeStruct(packed_b, BF),
            jax.ShapeDtypeStruct((4, D), F32),
            jax.ShapeDtypeStruct((1, FF), F32),
        ],
        scratch_shapes=[
            pltpu.VMEM((D, D), BF),
            pltpu.VMEM((2, D, F), BF),
            pltpu.VMEM((2, F, D), BF),
            pltpu.VMEM((D, F), BF),
            pltpu.VMEM((D, F), BF),
            pltpu.VMEM((n, D), BF),
            pltpu.VMEM((D, n), BF),
            pltpu.VMEM((D, n), BF),
            pltpu.VMEM((n, D), F32),
            pltpu.VMEM((n, D), F32),
            pltpu.VMEM((D, F), F32),
            pltpu.VMEM((D, F), F32),
            pltpu.SemaphoreType.DMA((6,)),
            pltpu.SemaphoreType.DMA((2, 17)),
            pltpu.SemaphoreType.DMA((20,)),
        ],
        compiler_params=pltpu.CompilerParams(vmem_limit_bytes=63 << 20),
        cost_estimate=pl.CostEstimate(
            flops=24 * n * D * FF,
            bytes_accessed=n * D * 16 + 12 * D * FF,
            transcendentals=n * FF,
        ),
        name="feed_forward",
    )(core, x, *mixed, g, mine, other, back_mine, back_other, vec, fb)


def last_kernel(x_ref, gh_ref, gain_ref, *refs):
    grads, w0, w1 = refs[:3], refs[3], refs[4]
    out_ref, sum_ref = refs[-2:]
    x = x_ref[...].astype(F32)
    c = x - jnp.mean(x, axis=1, keepdims=True)
    inv = lax.rsqrt(jnp.mean(c * c, axis=1, keepdims=True) + EPS)
    xhat = c * inv
    half = w1.shape[1] // 2
    one = dot(grads[0][...], w0[...], NT)
    one += dot(grads[1][...], w1[:, :half], NT)
    one += dot(grads[2][...], w1[:, half:], NT)
    e = one * gain_ref[...]
    m1 = jnp.mean(e, axis=1, keepdims=True)
    m2 = jnp.mean(e * xhat, axis=1, keepdims=True)
    out_ref[...] = gh_ref[...] + inv * (e - m1 - xhat * m2)
    sums = jnp.concatenate([jnp.sum(v, axis=0, keepdims=True) for v in (one * xhat, one)], axis=0)

    @pl.when(pl.program_id(0) == 0)
    def _():
        sum_ref[...] = sums

    @pl.when(pl.program_id(0) > 0)
    def _():
        sum_ref[...] += sums


def last(x, gh, gain, grads, weights, deps=(), T=512):
    n, D = x.shape
    block = pl.BlockSpec((T, D), lambda i: (i, 0))
    return pl.pallas_call(
        last_kernel,
        grid=(n // T,),
        in_specs=[block, block, pl.BlockSpec((1, D), lambda i: (0, 0))]
        + [block] * 3
        + [pl.BlockSpec(weight.shape, lambda i: (0, 0)) for weight in weights]
        + [pl.BlockSpec(memory_space=pl.ANY)] * len(deps),
        out_specs=[block, pl.BlockSpec((2, D), lambda i: (0, 0))],
        out_shape=[jax.ShapeDtypeStruct((n, D), F32), jax.ShapeDtypeStruct((2, D), F32)],
        compiler_params=pltpu.CompilerParams(vmem_limit_bytes=56 << 20),
        cost_estimate=pl.CostEstimate(
            flops=12 * n * D * D, bytes_accessed=n * D * 16, transcendentals=0
        ),
        name="input_gradient",
    )(x, gh, gain, *grads, *weights, *deps)


def project_kernel(order, rows, half, at, n1, mine, other, bias, *refs):
    qkv, w, sem = refs[-3:]
    me, core = at[0], at[1]

    @pl.when(pl.program_id(0) == 0)
    def _():
        copies = []
        for i, o in enumerate(order):
            row = pl.ds(pl.multiple_of((me ^ o) * rows, rows), rows)
            for src, part in ((mine, core), (other, 1 - core)):
                col = pl.ds(pl.multiple_of(part * half, 128), half)
                copies.append(
                    pltpu.make_async_copy(src.at[i, pl.ds(0, rows), :], w.at[row, col], sem.at[len(copies)])
                )
        for copy in copies:
            copy.start()
        for copy in copies:
            copy.wait()

    qkv[...] = (dot(n1[...], w[...], NN) + bias[...]).astype(BF)


def project(n1, mine, other, order, rows, bias, deps=(), T=512):
    n, D = n1.shape
    half = mine.shape[2]
    me, core = lax.axis_index("wide"), lax.axis_index("narrow") & 1
    if rows % 16:
        mine, other = [natural(p[:, :rows], order).reshape(-1, half) for p in (mine, other)]
        w = jnp.where(core == 0, jnp.concatenate([mine, other], 1), jnp.concatenate([other, mine], 1))
        return (dot(n1, w, NN) + bias).astype(BF), w
    anywhere = pl.BlockSpec(memory_space=pl.ANY)
    return pl.pallas_call(
        functools.partial(project_kernel, order, rows, half),
        grid=(n // T,),
        in_specs=[
            pl.BlockSpec(memory_space=pltpu.SMEM),
            pl.BlockSpec((T, D), lambda i: (i, 0)),
            anywhere,
            anywhere,
            pl.BlockSpec((1, 2 * half), lambda i: (0, 0)),
        ]
        + [anywhere] * len(deps),
        out_specs=[
            pl.BlockSpec((T, 2 * half), lambda i: (i, 0)),
            pl.BlockSpec((D, 2 * half), lambda i: (0, 0)),
        ],
        out_shape=[
            jax.ShapeDtypeStruct((n, 2 * half), BF),
            jax.ShapeDtypeStruct((D, 2 * half), BF),
        ],
        scratch_shapes=[pltpu.SemaphoreType.DMA((2 * len(order),))],
        compiler_params=pltpu.CompilerParams(vmem_limit_bytes=56 << 20),
        cost_estimate=pl.CostEstimate(
            flops=8 * n * D * half, bytes_accessed=n * D * 4 + n * half * 4, transcendentals=0
        ),
        name="project",
    )(jnp.stack([me, core]).astype(jnp.int32), n1, mine, other, bias, *deps)


def swap(x, axis, mask):
    size = lax.axis_size(axis)
    return lax.ppermute(x, axis, [(i, i ^ mask) for i in range(size)])


def bit_groups(size):
    top = size.bit_length() - 1
    cuts = [(0, 1)]
    low = 1
    while low < top:
        high = min(low + 2, top)
        cuts.append((low, high))
        low = high
    return cuts


def gather_wide(piece):
    size = lax.axis_size("wide")
    me = lax.axis_index("wide")
    stack, order = piece[None], [0]
    for low, high in reversed(bit_groups(size)):
        masks = [m << low for m in range(1 << (high - low))]
        stack = jnp.concatenate([stack] + [swap(stack, "wide", m) for m in masks[1:]])
        order = [o ^ m for m in masks for o in order]
    return stack, order


def natural(stack, order):
    size = len(order)
    me = lax.axis_index("wide")
    place = jnp.argsort(jnp.array(order))
    return jnp.take(stack, place[me ^ jnp.arange(size)], axis=0)


def gather(piece):
    mine, order = gather_wide(piece)
    return mine, swap(mine, "narrow", 1), order


def half_of(x, index, size, axis):
    return lax.dynamic_slice_in_dim(x, index * size, size, axis)


def add(*terms):
    total = terms[0].astype(F32)
    for term in terms[1:]:
        total = total + term.astype(F32)
    return total.astype(BF)


def scatter_wide(x):
    me = lax.axis_index("wide")
    size = x.shape[0]
    for low, high in bit_groups(size):
        ways = 1 << (high - low)
        mine = (me >> low) & (ways - 1)
        split = x.reshape((x.shape[0] // ways, ways) + x.shape[1:])
        got = [lax.dynamic_index_in_dim(split, mine, 1, keepdims=False)]
        for m in range(1, ways):
            sent = lax.dynamic_index_in_dim(split, mine ^ m, 1, keepdims=False)
            got.append(swap(sent, "wide", m << low))
        x = add(*got)
    return x[0]


def pick(x, low, high):
    me = lax.axis_index("wide")
    ways = 1 << (high - low)
    mine = (me >> low) & (ways - 1)
    split = [t.reshape((t.shape[0] // ways, ways) + t.shape[1:]) for t in x]
    return [add(*[lax.dynamic_index_in_dim(t, mine ^ m, 1, keepdims=False) for t in split]) for m in range(ways)]


def send(picked, low):
    return [picked[0]] + [swap(t, "wide", m << low) for m, t in enumerate(picked) if m]


def regroup(blocks, size):
    eight, depth, step = blocks.shape
    r = depth // 5
    blocks = blocks.reshape(eight, 5, r, step).transpose(0, 2, 1, 3).reshape(size, -1, 5, step)
    return blocks.transpose(0, 2, 1, 3).reshape(size, -1, step)


def regroup_back(blocks, size):
    eight, depth, step = blocks.shape
    blocks = blocks.transpose(1, 0, 2).reshape(depth, size, -1)
    return blocks.transpose(1, 0, 2)


def body(tokens, cotangent, row_kind, grad_mask, w_qkv, w_out, w_in, w_back, norm_gain, norm_shift, proj_bias, ffn_bias):
    rows, length, width = tokens.shape
    n = rows * length
    size = lax.axis_size("wide")
    share = width // size
    core = lax.axis_index("narrow") & 1
    packed = jnp.concatenate([norm_gain, norm_shift, proj_bias, ffn_bias.reshape(-1, share)])
    pairs = width // 128
    by_pair = w_qkv.reshape(share, 3, pairs, 128).transpose(0, 2, 1, 3).reshape(share, 3 * width)
    pieces = [half_of(by_pair[:, :768], core, 384, 1), half_of(by_pair[:, 768:], core, 768, 1)]
    extra = jnp.pad(packed.reshape(-1), (0, 16 * 384 - packed.size)).reshape(16, 384)
    pieces[0] = jnp.concatenate([pieces[0], extra])
    gathered = [gather(piece) for piece in pieces]
    small = natural(gathered[0][0][:, share:], gathered[0][2])
    small = small.reshape(size, -1)[:, : packed.size].reshape((size,) + packed.shape).astype(F32)
    hid = w_in.shape[1] // 2
    piece = jnp.concatenate(
        [half_of(w_out, core, width // 2, 1), half_of(w_in, core, hid, 1)]
        + [half_of(w_back[i * share : (i + 1) * share], core, width // 2, 1) for i in range(w_back.shape[0] // share)],
        axis=1,
    )
    mine = lax.all_gather(piece, "wide", axis=0, tiled=True)

    def back_half(gathered):
        chunks = gathered[:, width // 2 + hid :].reshape(size, share, -1, width // 2)
        return chunks.transpose(0, 2, 1, 3).reshape(-1, width // 2)

    by_column = small[:, :8].transpose(1, 0, 2).reshape(8, width)
    gains, shifts, biases = by_column[:2], by_column[2:4], by_column[4:8]
    ffn_bias_full = small[:, 8:].reshape(1, -1)
    x = tokens.reshape(n, width)
    inputs = x.astype(F32)
    centred = inputs - jnp.mean(inputs, axis=-1, keepdims=True)
    inv = lax.rsqrt(jnp.mean(centred * centred, axis=-1, keepdims=True) + EPS)
    normed_one = (centred * inv * gains[0] + shifts[0]).astype(BF)
    keep = jnp.where(row_kind[:, None] == 1, jnp.ones(grad_mask.shape, F32), grad_mask.astype(F32))
    g_ffn = (cotangent.astype(F32) * keep[:, :, None]).reshape(n, width).astype(BF)
    n1t = normed_one.T
    bias = jnp.stack([biases[0], jnp.zeros((width,), F32), biases[1]])
    bias = bias.reshape(3, pairs, 128).transpose(1, 0, 2).reshape(1, -1)
    qkv_a, w_a = project(normed_one, *gathered[0], share, bias[:, :768])
    mixed_a, lse_a = attn_fwd(qkv_a, 0, 2, rows)
    qkv_b, w_b = project(normed_one, *gathered[1], share, bias[:, 768:], deps=(mixed_a,))
    mixed_b, lse_b = attn_fwd(qkv_b, 0, 2, rows)
    mine = tie(mine, mixed_b)
    other = swap(mine, "narrow", 1)
    mixed_c, lse_c = attn_fwd(qkv_b, 2, 2, rows, deps=(mine,))
    vec = jnp.stack([gains[1], shifts[1], biases[2], biases[3]])
    direct = size == 8 and share % 16 == 0
    backs = (mine, other) if direct else (back_half(mine), back_half(other))
    at = core[None]
    layer_out, g_hidden, g_mixed, kept, sent, kept_b, sent_b, sums, ffn_sum = middle(
        at, x, (mixed_a, mixed_b, mixed_c), g_ffn, mine, other, *backs, direct, vec, ffn_bias_full
    )
    if size != 8:
        kept, sent, kept_b, sent_b = (
            regroup(kept, size), regroup(sent, size), regroup_back(kept_b, size), regroup_back(sent_b, size)
        )
    groups = [(bit, bit + 1) for bit in range(size.bit_length() - 1)]

    def finish(x, stage):
        for low, high in groups[stage:]:
            x = send(pick(x, low, high), low)
        return add(*x)[0]

    def step_on(x, stage):
        picked = pick(x, *groups[stage])
        return picked, send(picked, groups[stage][0])

    from_core = swap(sent, "narrow", 1)
    from_core_b = swap(sent_b, "narrow", 1)
    g_c, keep_c, send_c, sum_c = attn_bwd(at, qkv_b, 2, mixed_c, lse_c, g_mixed, 4, n1t, rows)
    both = add(kept, from_core)
    picked_b, x_b = step_on([kept_b, from_core_b], 0)
    summed = lax.psum_scatter(both.reshape(-1, both.shape[2]), "wide", scatter_dimension=0, tiled=True)
    from_core_c = swap(send_c, "narrow", 1)
    g_b, keep_d, send_d, sum_b = attn_bwd(
        at, qkv_b, 0, mixed_b, lse_b, g_mixed, 2, n1t, rows, deps=[both, keep_c] + picked_b
    )
    from_core_d = swap(send_d, "narrow", 1)
    picked_b, x_b = step_on(x_b, 1)
    tied = tie(from_core_c, keep_d)
    picked_c, x_c = step_on([t.reshape(size, share, -1) for t in (keep_c, tied)], 0)
    g_a, keep_e, send_e, sum_a = attn_bwd(
        at, qkv_a, 0, mixed_a, lse_a, g_mixed, 0, n1t, rows, deps=picked_b + picked_c + [keep_d]
    )
    from_core_e = swap(send_e, "narrow", 1)
    picked_b, x_b = step_on([x_b[0], tie(x_b[1], keep_e)], 2)
    picked_c, x_c = step_on([x_c[0], tie(x_c[1], keep_e)], 1)
    input_grad, last_sums = last(
        x, g_hidden, gains[:1], (g_a, g_b, g_c), (w_a, w_b), deps=picked_b + picked_c + [from_core_d]
    )
    column_sums = jnp.concatenate([t[0] for t in (sum_a, sum_b, sum_c)])
    column_sums = column_sums.reshape(pairs, 3, 128).transpose(1, 0, 2).reshape(3, width)
    by_column = jnp.stack(
        [last_sums[0], sums[0], last_sums[1], sums[1], column_sums[0], column_sums[2], sums[2], sums[3]]
    )
    by_column = by_column.reshape(8, size, share).transpose(1, 0, 2)
    small = jnp.concatenate([by_column, ffn_sum.reshape(size, -1, share)], axis=1).astype(BF).reshape(size, -1)
    count = small.shape[1]
    extra = -(-count // 768)
    small = jnp.pad(small, ((0, 0), (0, extra * 768 - count))).reshape(size, extra, 768)
    halves = [pick([t.reshape(size, share, -1) for t in ts], *groups[0]) for ts in ((keep_d, from_core_d), (keep_e, from_core_e))]
    picked = [
        jnp.concatenate([jnp.concatenate([d, e], axis=2), s], axis=1)
        for d, e, s in zip(*halves, pick([small], *groups[0]))
    ]
    x_b = [x_b[0], tie(x_b[1], last_sums)]
    x_c = [x_c[0], tie(x_c[1], last_sums)]
    block_b = finish(x_b, 3)
    early = jnp.concatenate([summed, block_b.reshape(-1, width // 2)], axis=0)
    early_y = swap(early, "narrow", 2)
    x_de = send(picked, 0)
    picked_c, x_c = step_on(x_c, 2)
    early = add(early, early_y)
    early_core = swap(early, "narrow", 1)
    x_de = [x_de[0], tie(x_de[1], early)]
    _, x_de = step_on(x_de, 1)
    x_de = [x_de[0], tie(x_de[1], early_core)]
    late = finish(x_de, 2)
    more = finish(x_c, 3)
    late = jnp.concatenate([late, jnp.pad(more, ((0, extra), (0, 0)))], axis=1)
    late = add(late, swap(late, "narrow", 2))
    late_core = swap(late, "narrow", 1)

    def ordered(mine, other):
        return [jnp.where(core == 0, mine, other), jnp.where(core == 0, other, mine)]

    left, right = ordered(early, early_core)
    five, step = 5 * share, width // 2
    share_out = jnp.concatenate([t[:share] for t in (left, right)], axis=1).astype(F32)
    share_in = jnp.concatenate(
        [t[i * share : (i + 1) * share] for t in (left, right) for i in range(1, 5)], axis=1
    ).astype(F32)
    share_back = jnp.concatenate([t[five:].reshape(step, -1).T for t in (left, right)], axis=1).astype(F32)
    small = late[share:, :768].astype(F32) + late_core[share:, :768].astype(F32)
    small = small.reshape(-1)[:count].reshape(-1, share)
    left, right = ordered(late[:share], late_core[:share])
    share_qkv = jnp.stack([left[:, 384:768], right[:, 384:768], left[:, :384], right[:, :384], left[:, 768:], right[:, 768:]], axis=1)
    share_qkv = share_qkv.reshape(share, pairs, 3, 128).transpose(0, 2, 1, 3).reshape(share, -1).astype(F32)
    return (
        layer_out.reshape(rows, length, width),
        input_grad.reshape(rows, length, width),
        share_qkv,
        share_out,
        share_in,
        share_back,
        small[:2],
        small[2:4],
        small[4:8],
        small[8:].reshape(-1),
    )


def solution(mesh):
    in_specs = (
        P(("wide", "narrow"), None, None),
        P(("wide", "narrow"), None, None),
        P(("wide", "narrow")),
        P(("wide", "narrow"), None),
        P("wide", None),
        P("wide", None),
        P("wide", None),
        P("wide", None),
        P(None, "wide"),
        P(None, "wide"),
        P(None, "wide"),
        P("wide"),
    )
    out_specs = (
        P(("wide", "narrow"), None, None),
        P(("wide", "narrow"), None, None),
        P("wide", None),
        P("wide", None),
        P("wide", None),
        P("wide", None),
        P(None, "wide"),
        P(None, "wide"),
        P(None, "wide"),
        P("wide"),
    )
    return jax.shard_map(body, mesh=mesh, in_specs=in_specs, out_specs=out_specs, check_vma=False)
```

```python
import functools

import jax
import jax.numpy as jnp
from jax import lax
from jax.experimental import pallas as pl
from jax.experimental.pallas import tpu as pltpu
from jax.sharding import PartitionSpec as P

HEADS = 12
F32 = jnp.float32
BF = jnp.bfloat16
EPS = 1e-05
ROOT = 0.7978845608028654
CUBIC = 0.044715
NN = (((1,), (0,)), ((), ()))
NT = (((1,), (1,)), ((), ()))
TN = (((0,), (0,)), ((), ()))


def dot(a, b, dims):
    return lax.dot_general(a, b, dims, preferred_element_type=F32)


def spread(x, lane):
    hi = x.astype(BF).astype(F32)
    rest = x - hi
    mid = rest.astype(BF).astype(F32)
    at = lane & 63
    zero = jnp.zeros_like(x)
    picked = jnp.where(at == 0, hi, jnp.where(at == 1, mid, jnp.where(at == 2, rest - mid, zero)))
    return picked.astype(BF)

def fwd_kernel(bq, x_ref, o_ref, l_ref, *_):
    length = x_ref.shape[0]
    lane = lax.broadcasted_iota(jnp.int32, (length, 128), 1)
    left = lane < 64
    lq = lax.broadcasted_iota(jnp.int32, (bq, 128), 1)
    leftq = lq < 64
    k = x_ref[:, 128:256]
    v = x_ref[:, 256:384].astype(F32)
    ones = jnp.ones_like(v)
    va = jnp.where(left, v, ones).astype(BF)
    vb = jnp.where(left, ones, v).astype(BF)
    for i in range(length // bq):
        q = x_ref[i * bq : (i + 1) * bq, :128].astype(F32) * 0.125
        zero = jnp.zeros_like(q)
        qa = jnp.where(leftq, q, zero).astype(BF)
        qb = jnp.where(leftq, zero, q).astype(BF)
        outs, peaks = [], []
        for qq, vv in ((qa, va), (qb, vb)):
            s = dot(qq, k, NT)
            m = jnp.max(s, axis=1, keepdims=True)
            p = jnp.exp(s - m).astype(BF)
            outs.append(dot(p, vv, NN))
            peaks.append(m)
        oa, ob = outs
        num = jnp.where(leftq, oa, ob)
        den = jnp.where(leftq, ob, oa)
        o_ref[i * bq : (i + 1) * bq, :] = (num / pltpu.roll(den, 64, 1)).astype(BF)
        lse = jnp.where(leftq, peaks[1], peaks[0]) + jnp.log(den)
        l_ref[i * bq : (i + 1) * bq, :] = spread(lse, lq)


def attn_fwd(qkv, first, pairs, rows, deps=(), bq=512):
    n = qkv.shape[0]
    length = n // rows
    width = pairs * 128
    out = pl.BlockSpec((length, 128), lambda s, p: (s, p))

    def kernel(x_ref, *refs):
        fwd_kernel(bq, x_ref, *refs[len(deps) :])

    return pl.pallas_call(
        kernel,
        grid=(rows, pairs),
        in_specs=[pl.BlockSpec((length, 384), lambda s, p: (s, first + p))]
        + [pl.BlockSpec(memory_space=pl.ANY)] * len(deps),
        out_specs=[out, out],
        out_shape=[jax.ShapeDtypeStruct((n, width), BF)] * 2,
        compiler_params=pltpu.CompilerParams(vmem_limit_bytes=56 << 20),
        cost_estimate=pl.CostEstimate(
            flops=30 * n * length * width,
            bytes_accessed=n * width * 10,
            transcendentals=n * length * width // 64,
        ),
        name="attention_forward",
    )(qkv, *deps)


def bwd_kernel(bq, at, x_ref, o_ref, l_ref, g_ref, n1t_ref, out_ref, keep_ref, send_ref, sum_ref, ak, av, dw):
    length = x_ref.shape[0]
    p, s, last = pl.program_id(0), pl.program_id(1), pl.num_programs(1) - 1
    lane = lax.broadcasted_iota(jnp.int32, (length, 128), 1)
    left = lane < 64
    lq = lax.broadcasted_iota(jnp.int32, (bq, 128), 1)
    leftq = lq < 64
    k = x_ref[:, 128:256].astype(F32)
    v = x_ref[:, 256:384].astype(F32)
    tail = jnp.where((lane & 63) < 3, -1.0, 0.0).astype(F32)
    zero = jnp.zeros_like(k)
    kx = (jnp.where(left, k, tail).astype(BF), jnp.where(left, tail, k).astype(BF))
    km = (jnp.where(left, k, zero).astype(BF), jnp.where(left, zero, k).astype(BF))
    vx = (jnp.where(left, v, tail).astype(BF), jnp.where(left, tail, v).astype(BF))
    for i in range(length // bq):
        here = slice(i * bq, (i + 1) * bq)
        q = x_ref[here, :128].astype(F32) * 0.125
        l = l_ref[here, :].astype(F32)
        g = g_ref[here, :].astype(F32)
        zq = jnp.zeros_like(q)
        prod = g * o_ref[here, :].astype(F32)
        da = jnp.sum(jnp.where(leftq, prod, zq), axis=1, keepdims=True)
        db = jnp.sum(jnp.where(leftq, zq, prod), axis=1, keepdims=True)
        d = spread(jnp.where(leftq, db, da), lq).astype(F32)
        qx = (jnp.where(leftq, q, l).astype(BF), jnp.where(leftq, l, q).astype(BF))
        qm = (jnp.where(leftq, q, zq).astype(BF), jnp.where(leftq, zq, q).astype(BF))
        gx = (jnp.where(leftq, g, d).astype(BF), jnp.where(leftq, d, g).astype(BF))
        gm = (jnp.where(leftq, g, zq).astype(BF), jnp.where(leftq, zq, g).astype(BF))
        gq = gk = gv = None
        for h in range(2):
            pr = jnp.exp(dot(kx[h], qx[h], NT))
            ds = (pr * dot(vx[h], gx[h], NT)).astype(BF)
            tv = dot(pr.astype(BF), gm[h], NN)
            tk = dot(ds, qm[h], NN)
            tq = dot(ds, km[h], TN)
            gq = tq if gq is None else gq + tq
            gk = tk if gk is None else gk + tk
            gv = tv if gv is None else gv + tv
        out_ref[here, :128] = (gq * 0.125).astype(BF)
        if i == 0:
            ak[...] = gk
            av[...] = gv
        else:
            ak[...] += gk
            av[...] += gv
    out_ref[:, 128:256] = ak[...].astype(BF)
    out_ref[:, 256:384] = av[...].astype(BF)
    got = out_ref[...]
    grad = dot(n1t_ref[...], got, NN)
    sums = jnp.sum(got.astype(F32), axis=0, keepdims=True)

    @pl.when(s == 0)
    def _():
        dw[...] = grad
        sum_ref[...] = jnp.broadcast_to(sums, (8, 384))

    @pl.when((s > 0) & (s < last))
    def _():
        dw[...] += grad

    @pl.when(s > 0)
    def _():
        sum_ref[...] += jnp.broadcast_to(sums, (8, 384))

    @pl.when((s == last) & (p == at[0]))
    def _():
        keep_ref[...] = (dw[...] + grad).astype(BF)

    @pl.when((s == last) & (p != at[0]))
    def _():
        send_ref[...] = (dw[...] + grad).astype(BF)


def attn_bwd(core, qkv, first, mixed, lse, gmixed, at_g, n1t, rows, deps=(), bq=256):
    n = qkv.shape[0]
    length = n // rows
    D = n1t.shape[0]
    pairs = 2
    block = pl.BlockSpec((length, 128), lambda p, s: (s, p))
    whole = pl.BlockSpec((D, 384), lambda p, s: (0, 0))

    def kernel(at, x, o, l, g, t, *refs):
        bwd_kernel(bq, at, x, o, l, g, t, *refs[len(deps) :])

    assert rows > 1
    return pl.pallas_call(
        kernel,
        grid=(pairs, rows),
        in_specs=[
            pl.BlockSpec(memory_space=pltpu.SMEM),
            pl.BlockSpec((length, 384), lambda p, s: (s, first + p)),
            block,
            block,
            pl.BlockSpec((length, 128), lambda p, s: (s, at_g + p)),
            pl.BlockSpec((D, length), lambda p, s: (0, s)),
        ]
        + [pl.BlockSpec(memory_space=pl.ANY)] * len(deps),
        out_specs=[
            pl.BlockSpec((length, 384), lambda p, s: (s, p)),
            whole,
            whole,
            pl.BlockSpec((8, 384), lambda p, s: (0, p)),
        ],
        out_shape=[
            jax.ShapeDtypeStruct((n, pairs * 384), BF),
            jax.ShapeDtypeStruct((D, 384), BF),
            jax.ShapeDtypeStruct((D, 384), BF),
            jax.ShapeDtypeStruct((8, pairs * 384), F32),
        ],
        scratch_shapes=[pltpu.VMEM((length, 128), F32)] * 2 + [pltpu.VMEM((D, 384), F32)],
        compiler_params=pltpu.CompilerParams(vmem_limit_bytes=56 << 20),
        cost_estimate=pl.CostEstimate(
            flops=56 * n * length * pairs * 128,
            bytes_accessed=n * pairs * 128 * 18,
            transcendentals=n * length * pairs * 2,
        ),
        name="attention_backward",
    )(core, qkv, mixed, lse, gmixed, n1t, *deps)


def tie_kernel(a, b, out):
    pass


def tie(x, after):
    anywhere = pl.BlockSpec(memory_space=pl.ANY)
    return pl.pallas_call(
        tie_kernel,
        in_specs=[anywhere] * 2,
        out_specs=anywhere,
        out_shape=jax.ShapeDtypeStruct(x.shape, x.dtype),
        input_output_aliases={0: 0},
        name="tie",
    )(x, after)


def mid_kernel(T, direct, at, x_any, m0_any, m1_any, m2_any, g, mine, other, back_mine, back_other, vec_ref, fb_ref,
               out_ref, gh_ref, gm_ref, keep, send, keep_b, send_b, sum_ref, fs_ref,
               wo, wi_s, wb_s, gi_s, gb_s, n2, n2t, gt, xh, acc, ai, ab, sem, wsem, gsem):
    f, nf = pl.program_id(0), pl.num_programs(0)
    core = at[0]
    n, D = n2.shape
    F = wi_s.shape[2]
    blocks, half, r = n // T, D // 2, D // 8
    at_back = mine.shape[1] - (half // r) * half
    x_ref, m_ref, gtw = out_ref, gm_ref, gh_ref

    left = pl.ds(pl.multiple_of(core * half, 128), half)
    right = pl.ds(pl.multiple_of((1 - core) * half, 128), half)

    def back(step, slot):
        if not direct:
            rows = pl.ds(pl.multiple_of(step * F, 128), F)
            return [(back_mine.at[rows, :], wb_s.at[slot, :, left]), (back_other.at[rows, :], wb_s.at[slot, :, right])]
        out = []
        for k in range(F // half):
            rows = pl.ds(pl.multiple_of((step * (F // half) + k) * r, r), r)
            for t in range(half // r):
                cols = pl.ds(at_back + t * half, half)
                to = slice(k * half + t * r, k * half + (t + 1) * r)
                out.append((mine.at[rows, cols], wb_s.at[slot, to, left]))
                out.append((other.at[rows, cols], wb_s.at[slot, to, right]))
        return out

    def inner(step):
        return pl.ds(pl.multiple_of(half + lax.rem(step, nf // 2) * F, 128), F)

    def fetch(step, slot):
        @pl.when(step // (nf // 2) == core)
        def _():
            pltpu.make_async_copy(mine.at[:, inner(step)], wi_s.at[slot], wsem.at[slot, 0]).start()

        @pl.when(step // (nf // 2) != core)
        def _():
            pltpu.make_async_copy(other.at[:, inner(step)], wi_s.at[slot], wsem.at[slot, 0]).start()

        for i, (src, to) in enumerate(back(step, slot)):
            pltpu.make_async_copy(src, to, wsem.at[slot, 1 + i]).start()

    def grads(step):
        part, local = step // (nf // 2), lax.rem(step, nf // 2)
        out = []
        per = F // half
        for w in range(8):
            for k in range(per):
                row = pl.multiple_of(r + (local * per + k) * r, r)
                src = gi_s.at[w * r : (w + 1) * r, k * half : (k + 1) * half]
                out.append((part, (keep, send), w, pl.ds(row, r), src))
        for k in range(per):
            for h in range(2):
                src = gb_s.at[h * half : (h + 1) * half, k * half : (k + 1) * half]
                out.append((h, (keep_b, send_b), step * per + k, pl.ds(0, half), src))
        return out

    def store(copies):
        for i, (part, to, w, rows, src) in enumerate(copies):
            @pl.when(part == core)
            def _():
                pltpu.make_async_copy(src, to[0].at[w, rows, :], gsem.at[i]).start()

            @pl.when(part != core)
            def _():
                pltpu.make_async_copy(src, to[1].at[w, rows, :], gsem.at[i]).start()

    def settle(copies):
        for i, (part, to, w, rows, src) in enumerate(copies):
            pltpu.make_async_copy(src, to[0].at[w, rows, :], gsem.at[i]).wait()

    slot = lax.rem(f, 2)

    @pl.when(f == 0)
    def _():
        cx = pltpu.make_async_copy(x_any, x_ref, sem.at[0])
        cx.start()
        start = 0
        cm = []
        for j, a in enumerate((m0_any, m1_any, m2_any)):
            w = a.shape[1]
            cm.append(pltpu.make_async_copy(a, m_ref.at[:, pl.ds(start, w)], sem.at[1 + j]))
            start += w
        cm.append(pltpu.make_async_copy(mine.at[:, pl.ds(0, half)], wo.at[:, left], sem.at[4]))
        cm.append(pltpu.make_async_copy(other.at[:, pl.ds(0, half)], wo.at[:, right], sem.at[5]))
        for copy in cm:
            copy.start()
        fetch(0, 0)
        for copy in [cx] + cm:
            copy.wait()

        @pl.loop(0, blocks)
        def _(i):
            at_t = pl.ds(pl.multiple_of(i * T, T), T)
            hidden = x_ref[at_t, :].astype(F32) + dot(m_ref[at_t, :], wo[...], NN) + vec_ref[2:3, :]
            c = hidden - jnp.mean(hidden, axis=1, keepdims=True)
            inv = lax.rsqrt(jnp.mean(c * c, axis=1, keepdims=True) + EPS)
            nn = (c * inv * vec_ref[0:1, :] + vec_ref[1:2, :]).astype(BF)
            acc[at_t, :] = hidden + vec_ref[3:4, :]
            xh[at_t, :] = c
            n2[at_t, :] = nn
            n2t[:, at_t] = nn.T
            gt[:, at_t] = g[at_t, :].T

    @pl.when(f < nf - 1)
    def _():
        fetch(f + 1, 1 - slot)

    pltpu.make_async_copy(mine.at[:, inner(f)], wi_s.at[slot], wsem.at[slot, 0]).wait()
    for i, (src, to) in enumerate(back(f, slot)):
        pltpu.make_async_copy(src, to, wsem.at[slot, 1 + i]).wait()
    wi_ref, wb_ref = wi_s.at[slot], wb_s.at[slot]
    fs = None
    for i in range(blocks):
        at_t = pl.ds(i * T, T)
        pre = dot(n2[at_t, :], wi_ref[...], NN) + fb_ref[...]
        ga = dot(g[at_t, :], wb_ref[...], NT)
        sq = pre * pre
        t = jnp.tanh(pre * (ROOT + (ROOT * CUBIC) * sq))
        part = 0.5 * pre
        act = (part + part * t).astype(BF)
        slope = (0.5 + 0.5 * t) + part * (1.0 - t * t) * (ROOT + (3 * ROOT * CUBIC) * sq)
        gp = (ga * slope).astype(BF)
        s = jnp.sum(gp.astype(F32), axis=0, keepdims=True)
        fs = s if fs is None else fs + s
        a = dot(n2t[:, i * T : (i + 1) * T], gp, NN)
        b = dot(gt[:, i * T : (i + 1) * T], act, NN)
        if i == 0:
            ai[...] = a
            ab[...] = b
        elif i < blocks - 1:
            ai[...] += a
            ab[...] += b
        else:
            @pl.when(f > 0)
            def _():
                settle(grads(f - 1))

            gi_s[...] = (ai[...] + a).astype(BF)
            gb_s[...] = (ab[...] + b).astype(BF)
            store(grads(f))
        acc[at_t, :] += dot(act, wb_ref[...], NN)
        gtwo = dot(gp, wi_ref[...], NT)

        @pl.when(f == 0)
        def _():
            gtw[at_t, :] = gtwo

        @pl.when(f > 0)
        def _():
            gtw[at_t, :] += gtwo

    fs_ref[...] = fs

    @pl.when(f == nf - 1)
    def _():
        sum_ref[...] = jnp.zeros_like(sum_ref)
        ai[...] = jnp.zeros_like(ai)

        @pl.loop(0, blocks)
        def _(i):
            at_t = pl.ds(pl.multiple_of(i * T, T), T)
            out_ref[at_t, :] = acc[at_t, :].astype(BF)
            gtwo, c = gtw[at_t, :], xh[at_t, :]
            inv = lax.rsqrt(jnp.mean(c * c, axis=1, keepdims=True) + EPS)
            xhat = c * inv
            e = gtwo * vec_ref[0:1, :]
            m1 = jnp.mean(e, axis=1, keepdims=True)
            m2 = jnp.mean(e * xhat, axis=1, keepdims=True)
            gg = g[at_t, :].astype(F32)
            gh = gg + inv * (e - m1 - xhat * m2)
            gh_ref[at_t, :] = gh
            ga = gh.astype(BF)
            ai[...] += dot(m_ref[at_t, :], ga, TN)
            gm_ref[at_t, :] = dot(ga, wo[...], NT).astype(BF)
            rows = (gtwo * xhat, gtwo, ga.astype(F32), gg)
            sum_ref[...] += jnp.concatenate([jnp.sum(v, axis=0, keepdims=True) for v in rows], axis=0)

        settle(grads(f))
        gi_s[...] = ai[...].astype(BF)
        last_ones = [
            (h, (keep, send), w, pl.ds(0, r), gi_s.at[w * r : (w + 1) * r, h * half : (h + 1) * half])
            for w in range(8)
            for h in range(2)
        ]
        store(last_ones)
        settle(last_ones)


def middle(core, x, mixed, g, mine, other, back_mine, back_other, direct, vec, fb, F=768, T=512):
    n, D = x.shape
    FF = fb.shape[1]
    one = pl.Buffered(1)

    def full(shape):
        return pl.BlockSpec(shape, lambda f: (0, 0), pipeline_mode=one)

    anywhere = pl.BlockSpec(memory_space=pl.ANY)
    packed = (8, D // 8 + FF // 8, D // 2)
    packed_b = (8, D // 2, FF // 8)
    return pl.pallas_call(
        functools.partial(mid_kernel, T, direct),
        grid=(FF // F,),
        in_specs=[pl.BlockSpec(memory_space=pltpu.SMEM)]
        + [anywhere] * 4
        + [full((n, D))]
        + [anywhere] * 4
        + [full((4, D)), pl.BlockSpec((1, F), lambda f: (0, f))],
        out_specs=[full((n, D)), full((n, D)), full((n, D))] + [anywhere] * 4
        + [full((4, D)), pl.BlockSpec((1, F), lambda f: (0, f))],
        out_shape=[
            jax.ShapeDtypeStruct((n, D), BF),
            jax.ShapeDtypeStruct((n, D), F32),
            jax.ShapeDtypeStruct((n, D), BF),
            jax.ShapeDtypeStruct(packed, BF),
            jax.ShapeDtypeStruct(packed, BF),
            jax.ShapeDtypeStruct(packed_b, BF),
            jax.ShapeDtypeStruct(packed_b, BF),
            jax.ShapeDtypeStruct((4, D), F32),
            jax.ShapeDtypeStruct((1, FF), F32),
        ],
        scratch_shapes=[
            pltpu.VMEM((D, D), BF),
            pltpu.VMEM((2, D, F), BF),
            pltpu.VMEM((2, F, D), BF),
            pltpu.VMEM((D, F), BF),
            pltpu.VMEM((D, F), BF),
            pltpu.VMEM((n, D), BF),
            pltpu.VMEM((D, n), BF),
            pltpu.VMEM((D, n), BF),
            pltpu.VMEM((n, D), F32),
            pltpu.VMEM((n, D), F32),
            pltpu.VMEM((D, F), F32),
            pltpu.VMEM((D, F), F32),
            pltpu.SemaphoreType.DMA((6,)),
            pltpu.SemaphoreType.DMA((2, 17)),
            pltpu.SemaphoreType.DMA((20,)),
        ],
        compiler_params=pltpu.CompilerParams(vmem_limit_bytes=63 << 20),
        cost_estimate=pl.CostEstimate(
            flops=24 * n * D * FF,
            bytes_accessed=n * D * 16 + 12 * D * FF,
            transcendentals=n * FF,
        ),
        name="feed_forward",
    )(core, x, *mixed, g, mine, other, back_mine, back_other, vec, fb)


def last_kernel(x_ref, gh_ref, gain_ref, *refs):
    grads, w0, w1 = refs[:3], refs[3], refs[4]
    out_ref, sum_ref = refs[-2:]
    x = x_ref[...].astype(F32)
    c = x - jnp.mean(x, axis=1, keepdims=True)
    inv = lax.rsqrt(jnp.mean(c * c, axis=1, keepdims=True) + EPS)
    xhat = c * inv
    half = w1.shape[1] // 2
    one = dot(grads[0][...], w0[...], NT)
    one += dot(grads[1][...], w1[:, :half], NT)
    one += dot(grads[2][...], w1[:, half:], NT)
    e = one * gain_ref[...]
    m1 = jnp.mean(e, axis=1, keepdims=True)
    m2 = jnp.mean(e * xhat, axis=1, keepdims=True)
    out_ref[...] = gh_ref[...] + inv * (e - m1 - xhat * m2)
    sums = jnp.concatenate([jnp.sum(v, axis=0, keepdims=True) for v in (one * xhat, one)], axis=0)

    @pl.when(pl.program_id(0) == 0)
    def _():
        sum_ref[...] = sums

    @pl.when(pl.program_id(0) > 0)
    def _():
        sum_ref[...] += sums


def last(x, gh, gain, grads, weights, deps=(), T=512):
    n, D = x.shape
    block = pl.BlockSpec((T, D), lambda i: (i, 0))
    return pl.pallas_call(
        last_kernel,
        grid=(n // T,),
        in_specs=[block, block, pl.BlockSpec((1, D), lambda i: (0, 0))]
        + [block] * 3
        + [pl.BlockSpec(weight.shape, lambda i: (0, 0)) for weight in weights]
        + [pl.BlockSpec(memory_space=pl.ANY)] * len(deps),
        out_specs=[block, pl.BlockSpec((2, D), lambda i: (0, 0))],
        out_shape=[jax.ShapeDtypeStruct((n, D), F32), jax.ShapeDtypeStruct((2, D), F32)],
        compiler_params=pltpu.CompilerParams(vmem_limit_bytes=56 << 20),
        cost_estimate=pl.CostEstimate(
            flops=12 * n * D * D, bytes_accessed=n * D * 16, transcendentals=0
        ),
        name="input_gradient",
    )(x, gh, gain, *grads, *weights, *deps)


def project_kernel(order, rows, half, at, n1, mine, other, bias, *refs):
    qkv, w, sem = refs[-3:]
    me, core = at[0], at[1]

    @pl.when(pl.program_id(0) == 0)
    def _():
        copies = []
        for i, o in enumerate(order):
            row = pl.ds(pl.multiple_of((me ^ o) * rows, rows), rows)
            for src, part in ((mine, core), (other, 1 - core)):
                col = pl.ds(pl.multiple_of(part * half, 128), half)
                copies.append(
                    pltpu.make_async_copy(src.at[i, pl.ds(0, rows), :], w.at[row, col], sem.at[len(copies)])
                )
        for copy in copies:
            copy.start()
        for copy in copies:
            copy.wait()

    qkv[...] = (dot(n1[...], w[...], NN) + bias[...]).astype(BF)


def project(n1, mine, other, order, rows, bias, deps=(), T=512):
    n, D = n1.shape
    half = mine.shape[2]
    me, core = lax.axis_index("wide"), lax.axis_index("narrow") & 1
    if rows % 16:
        mine, other = [natural(p[:, :rows], order).reshape(-1, half) for p in (mine, other)]
        w = jnp.where(core == 0, jnp.concatenate([mine, other], 1), jnp.concatenate([other, mine], 1))
        return (dot(n1, w, NN) + bias).astype(BF), w
    anywhere = pl.BlockSpec(memory_space=pl.ANY)
    return pl.pallas_call(
        functools.partial(project_kernel, order, rows, half),
        grid=(n // T,),
        in_specs=[
            pl.BlockSpec(memory_space=pltpu.SMEM),
            pl.BlockSpec((T, D), lambda i: (i, 0)),
            anywhere,
            anywhere,
            pl.BlockSpec((1, 2 * half), lambda i: (0, 0)),
        ]
        + [anywhere] * len(deps),
        out_specs=[
            pl.BlockSpec((T, 2 * half), lambda i: (i, 0)),
            pl.BlockSpec((D, 2 * half), lambda i: (0, 0)),
        ],
        out_shape=[
            jax.ShapeDtypeStruct((n, 2 * half), BF),
            jax.ShapeDtypeStruct((D, 2 * half), BF),
        ],
        scratch_shapes=[pltpu.SemaphoreType.DMA((2 * len(order),))],
        compiler_params=pltpu.CompilerParams(vmem_limit_bytes=56 << 20),
        cost_estimate=pl.CostEstimate(
            flops=8 * n * D * half, bytes_accessed=n * D * 4 + n * half * 4, transcendentals=0
        ),
        name="project",
    )(jnp.stack([me, core]).astype(jnp.int32), n1, mine, other, bias, *deps)


def swap(x, axis, mask):
    size = lax.axis_size(axis)
    return lax.ppermute(x, axis, [(i, i ^ mask) for i in range(size)])


def bit_groups(size):
    top = size.bit_length() - 1
    cuts = [(0, 1)]
    low = 1
    while low < top:
        high = min(low + 2, top)
        cuts.append((low, high))
        low = high
    return cuts


def gather_wide(piece):
    size = lax.axis_size("wide")
    me = lax.axis_index("wide")
    stack, order = piece[None], [0]
    for low, high in reversed(bit_groups(size)):
        masks = [m << low for m in range(1 << (high - low))]
        stack = jnp.concatenate([stack] + [swap(stack, "wide", m) for m in masks[1:]])
        order = [o ^ m for m in masks for o in order]
    return stack, order


def natural(stack, order):
    size = len(order)
    me = lax.axis_index("wide")
    place = jnp.argsort(jnp.array(order))
    return jnp.take(stack, place[me ^ jnp.arange(size)], axis=0)


def gather(piece):
    mine, order = gather_wide(piece)
    return mine, swap(mine, "narrow", 1), order


def half_of(x, index, size, axis):
    return lax.dynamic_slice_in_dim(x, index * size, size, axis)


def add(*terms):
    total = terms[0].astype(F32)
    for term in terms[1:]:
        total = total + term.astype(F32)
    return total.astype(BF)


def scatter_wide(x):
    me = lax.axis_index("wide")
    size = x.shape[0]
    for low, high in bit_groups(size):
        ways = 1 << (high - low)
        mine = (me >> low) & (ways - 1)
        split = x.reshape((x.shape[0] // ways, ways) + x.shape[1:])
        got = [lax.dynamic_index_in_dim(split, mine, 1, keepdims=False)]
        for m in range(1, ways):
            sent = lax.dynamic_index_in_dim(split, mine ^ m, 1, keepdims=False)
            got.append(swap(sent, "wide", m << low))
        x = add(*got)
    return x[0]


def pick(x, low, high):
    me = lax.axis_index("wide")
    ways = 1 << (high - low)
    mine = (me >> low) & (ways - 1)
    split = [t.reshape((t.shape[0] // ways, ways) + t.shape[1:]) for t in x]
    return [add(*[lax.dynamic_index_in_dim(t, mine ^ m, 1, keepdims=False) for t in split]) for m in range(ways)]


def send(picked, low):
    return [picked[0]] + [swap(t, "wide", m << low) for m, t in enumerate(picked) if m]


def regroup(blocks, size):
    eight, depth, step = blocks.shape
    r = depth // 5
    blocks = blocks.reshape(eight, 5, r, step).transpose(0, 2, 1, 3).reshape(size, -1, 5, step)
    return blocks.transpose(0, 2, 1, 3).reshape(size, -1, step)


def regroup_back(blocks, size):
    eight, depth, step = blocks.shape
    blocks = blocks.transpose(1, 0, 2).reshape(depth, size, -1)
    return blocks.transpose(1, 0, 2)


def body(tokens, cotangent, row_kind, grad_mask, w_qkv, w_out, w_in, w_back, norm_gain, norm_shift, proj_bias, ffn_bias):
    rows, length, width = tokens.shape
    n = rows * length
    size = lax.axis_size("wide")
    share = width // size
    core = lax.axis_index("narrow") & 1
    packed = jnp.concatenate([norm_gain, norm_shift, proj_bias, ffn_bias.reshape(-1, share)])
    pairs = width // 128
    by_pair = w_qkv.reshape(share, 3, pairs, 128).transpose(0, 2, 1, 3).reshape(share, 3 * width)
    pieces = [half_of(by_pair[:, :768], core, 384, 1), half_of(by_pair[:, 768:], core, 768, 1)]
    extra = jnp.pad(packed.reshape(-1), (0, 16 * 384 - packed.size)).reshape(16, 384)
    pieces[0] = jnp.concatenate([pieces[0], extra])
    gathered = [gather(piece) for piece in pieces]
    small = natural(gathered[0][0][:, share:], gathered[0][2])
    small = small.reshape(size, -1)[:, : packed.size].reshape((size,) + packed.shape).astype(F32)
    hid = w_in.shape[1] // 2
    piece = jnp.concatenate(
        [half_of(w_out, core, width // 2, 1), half_of(w_in, core, hid, 1)]
        + [half_of(w_back[i * share : (i + 1) * share], core, width // 2, 1) for i in range(w_back.shape[0] // share)],
        axis=1,
    )
    mine = lax.all_gather(piece, "wide", axis=0, tiled=True)

    def back_half(gathered):
        chunks = gathered[:, width // 2 + hid :].reshape(size, share, -1, width // 2)
        return chunks.transpose(0, 2, 1, 3).reshape(-1, width // 2)

    by_column = small[:, :8].transpose(1, 0, 2).reshape(8, width)
    gains, shifts, biases = by_column[:2], by_column[2:4], by_column[4:8]
    ffn_bias_full = small[:, 8:].reshape(1, -1)
    x = tokens.reshape(n, width)
    inputs = x.astype(F32)
    centred = inputs - jnp.mean(inputs, axis=-1, keepdims=True)
    inv = lax.rsqrt(jnp.mean(centred * centred, axis=-1, keepdims=True) + EPS)
    normed_one = (centred * inv * gains[0] + shifts[0]).astype(BF)
    keep = jnp.where(row_kind[:, None] == 1, jnp.ones(grad_mask.shape, F32), grad_mask.astype(F32))
    g_ffn = (cotangent.astype(F32) * keep[:, :, None]).reshape(n, width).astype(BF)
    n1t = normed_one.T
    bias = jnp.stack([biases[0], jnp.zeros((width,), F32), biases[1]])
    bias = bias.reshape(3, pairs, 128).transpose(1, 0, 2).reshape(1, -1)
    qkv_a, w_a = project(normed_one, *gathered[0], share, bias[:, :768])
    mixed_a, lse_a = attn_fwd(qkv_a, 0, 2, rows)
    qkv_b, w_b = project(normed_one, *gathered[1], share, bias[:, 768:], deps=(mixed_a,))
    mixed_b, lse_b = attn_fwd(qkv_b, 0, 2, rows)
    mine = tie(mine, mixed_b)
    other = swap(mine, "narrow", 1)
    mixed_c, lse_c = attn_fwd(qkv_b, 2, 2, rows, deps=(mine,))
    vec = jnp.stack([gains[1], shifts[1], biases[2], biases[3]])
    direct = size == 8 and share % 16 == 0
    backs = (mine, other) if direct else (back_half(mine), back_half(other))
    at = core[None]
    layer_out, g_hidden, g_mixed, kept, sent, kept_b, sent_b, sums, ffn_sum = middle(
        at, x, (mixed_a, mixed_b, mixed_c), g_ffn, mine, other, *backs, direct, vec, ffn_bias_full
    )
    if size != 8:
        kept, sent, kept_b, sent_b = (
            regroup(kept, size), regroup(sent, size), regroup_back(kept_b, size), regroup_back(sent_b, size)
        )
    groups = [(bit, bit + 1) for bit in range(size.bit_length() - 1)]

    def finish(x, stage):
        for low, high in groups[stage:]:
            x = send(pick(x, low, high), low)
        return add(*x)[0]

    def step_on(x, stage):
        picked = pick(x, *groups[stage])
        return picked, send(picked, groups[stage][0])

    from_core = swap(sent, "narrow", 1)
    from_core_b = swap(sent_b, "narrow", 1)
    g_c, keep_c, send_c, sum_c = attn_bwd(at, qkv_b, 2, mixed_c, lse_c, g_mixed, 4, n1t, rows)
    both = add(kept, from_core)
    picked_b, x_b = step_on([kept_b, from_core_b], 0)
    summed = lax.psum_scatter(both.reshape(-1, both.shape[2]), "wide", scatter_dimension=0, tiled=True)
    from_core_c = swap(send_c, "narrow", 1)
    g_b, keep_d, send_d, sum_b = attn_bwd(
        at, qkv_b, 0, mixed_b, lse_b, g_mixed, 2, n1t, rows, deps=[both, keep_c] + picked_b
    )
    from_core_d = swap(send_d, "narrow", 1)
    picked_b, x_b = step_on(x_b, 1)
    tied = tie(from_core_c, keep_d)
    picked_c, x_c = step_on([t.reshape(size, share, -1) for t in (keep_c, tied)], 0)
    g_a, keep_e, send_e, sum_a = attn_bwd(
        at, qkv_a, 0, mixed_a, lse_a, g_mixed, 0, n1t, rows, deps=picked_b + picked_c + [keep_d]
    )
    from_core_e = swap(send_e, "narrow", 1)
    picked_b, x_b = step_on([x_b[0], tie(x_b[1], keep_e)], 2)
    picked_c, x_c = step_on([x_c[0], tie(x_c[1], keep_e)], 1)
    input_grad, last_sums = last(
        x, g_hidden, gains[:1], (g_a, g_b, g_c), (w_a, w_b), deps=picked_b + picked_c + [from_core_d]
    )
    column_sums = jnp.concatenate([t[0] for t in (sum_a, sum_b, sum_c)])
    column_sums = column_sums.reshape(pairs, 3, 128).transpose(1, 0, 2).reshape(3, width)
    by_column = jnp.stack(
        [last_sums[0], sums[0], last_sums[1], sums[1], column_sums[0], column_sums[2], sums[2], sums[3]]
    )
    by_column = by_column.reshape(8, size, share).transpose(1, 0, 2)
    small = jnp.concatenate([by_column, ffn_sum.reshape(size, -1, share)], axis=1).astype(BF).reshape(size, -1)
    count = small.shape[1]
    extra = -(-count // 6144) * 8
    small = jnp.pad(small, ((0, 0), (0, extra * 768 - count))).reshape(size, extra, 768)
    halves = [pick([t.reshape(size, share, -1) for t in ts], *groups[0]) for ts in ((keep_d, from_core_d), (keep_e, from_core_e))]
    picked = [
        jnp.concatenate([jnp.concatenate([d, e], axis=2), s], axis=1)
        for d, e, s in zip(*halves, pick([small], *groups[0]))
    ]
    x_b = [x_b[0], tie(x_b[1], last_sums)]
    x_c = [x_c[0], tie(x_c[1], last_sums)]
    block_b = finish(x_b, 3)
    early = jnp.concatenate([summed, block_b.reshape(-1, width // 2)], axis=0)
    early_y = swap(early, "narrow", 2)
    x_de = send(picked, 0)
    picked_c, x_c = step_on(x_c, 2)
    early = add(early, early_y)
    early_core = swap(early, "narrow", 1)
    x_de = [x_de[0], tie(x_de[1], early)]
    _, x_de = step_on(x_de, 1)
    x_de = [x_de[0], tie(x_de[1], early_core)]
    late = finish(x_de, 2)
    more = finish(x_c, 3)
    late = jnp.concatenate([late, jnp.pad(more, ((0, extra), (0, 0)))], axis=1)
    late = add(late, swap(late, "narrow", 2))
    late_core = swap(late, "narrow", 1)

    def ordered(mine, other):
        return [jnp.where(core == 0, mine, other), jnp.where(core == 0, other, mine)]

    left, right = ordered(early, early_core)
    five, step = 5 * share, width // 2
    share_out = jnp.concatenate([t[:share] for t in (left, right)], axis=1).astype(F32)
    share_in = jnp.concatenate(
        [t[i * share : (i + 1) * share] for t in (left, right) for i in range(1, 5)], axis=1
    ).astype(F32)
    share_back = jnp.concatenate([t[five:].reshape(step, -1).T for t in (left, right)], axis=1).astype(F32)
    small = late[share:, :768].astype(F32) + late_core[share:, :768].astype(F32)
    small = small.reshape(-1)[:count].reshape(-1, share)
    left, right = ordered(late[:share], late_core[:share])
    share_qkv = jnp.stack([left[:, 384:768], right[:, 384:768], left[:, :384], right[:, :384], left[:, 768:], right[:, 768:]], axis=1)
    share_qkv = share_qkv.reshape(share, pairs, 3, 128).transpose(0, 2, 1, 3).reshape(share, -1).astype(F32)
    return (
        layer_out.reshape(rows, length, width),
        input_grad.reshape(rows, length, width),
        share_qkv,
        share_out,
        share_in,
        share_back,
        small[:2],
        small[2:4],
        small[4:8],
        small[8:].reshape(-1),
    )


def solution(mesh):
    in_specs = (
        P(("wide", "narrow"), None, None),
        P(("wide", "narrow"), None, None),
        P(("wide", "narrow")),
        P(("wide", "narrow"), None),
        P("wide", None),
        P("wide", None),
        P("wide", None),
        P("wide", None),
        P(None, "wide"),
        P(None, "wide"),
        P(None, "wide"),
        P("wide"),
    )
    out_specs = (
        P(("wide", "narrow"), None, None),
        P(("wide", "narrow"), None, None),
        P("wide", None),
        P("wide", None),
        P("wide", None),
        P("wide", None),
        P(None, "wide"),
        P(None, "wide"),
        P(None, "wide"),
        P("wide"),
    )
    return jax.shard_map(body, mesh=mesh, in_specs=in_specs, out_specs=out_specs, check_vma=False)
```
